32 devices in a mesh: dp: 8 (over z, core), ctx: 4 (over y, x).
Axes of the slice: x: 2, y: 2, z: 4, core: 2. Of those that a mesh axis runs over, the one named last changes fastest.
Arguments:
- hidden: bfloat16 [8, 512, 5120], P('dp', 'ctx'), may hold values from -6 to 6
- queries: bfloat16 [8, 512, 4096], P('dp', 'ctx'), may hold values from -6 to 6
- key_states: bfloat16 [8, 512, 512], P('dp', 'ctx'), may hold values from -6 to 6
- out_grad: bfloat16 [8, 512, 4096], P('dp', 'ctx'), may hold values from -6 to 6
- w_value: bfloat16 [5120, 512], replicated, may hold values from -0.078125 to 0.078125
- q_gain: float32 [128], replicated, may hold values from 0.1 to 1.9
- k_gain: float32 [128], replicated, may hold values from 0.1 to 1.9
- dest_rows: int32 [8, 512], P('dp', 'ctx'), may hold values from 0 to 511, as said below
- doc_ids: int32 [8, 512], P('dp', 'ctx'), may hold values from 0 to 3, never falling along the last dimension, each value on 1 to 256 neighbouring positions
Outputs:
- hidden_grad: bfloat16 [8, 512, 5120], P('dp', 'ctx')
- query_grad: bfloat16 [8, 512, 4096], P('dp', 'ctx')
- key_grad: bfloat16 [8, 512, 512], P('dp', 'ctx')
- weight_grad: float32 [5120, 512], P(('dp', 'ctx'))
The draws below stay inside these ranges and needn't reach their ends.
Inputs may be any that keep to these rules, and one draw needn't show every extreme that they name: `dest_rows`: within each data group the entries are a permutation of the slab's rows; the 128 entries of one block of arrival rows name exactly 64 or no rows of each block of 128 slab rows. `doc_ids`: ids never fall along a slab.
All inputs are finite; a program needn't handle non-finite values.
Results may differ from the reference program's by a relative error of at most 0.017.
Values may be sent and summed in bfloat16 or wider, within the bound.
No kernel may reach another device: no remote copies, remote signals or barrier semaphores. Data moves between devices by JAX's collectives and lax.ppermute only.
A program may use at most 128 MiB of HBM per device.

```python
import math
import jax
import jax.numpy as jnp
import numpy as np
from jax import lax

D = 5120
QH = 32
KVH = 4
HD = 128
TOK_DEV = 128
DOCS = 4
SLAB = 512
CAP = 64
DOC_MOST = 256
N_DP = 8
N_CTX = 4


def draw_dest_rows(key, part):

    def arrange(group_key):
        offsets = jax.random.permutation(jax.random.fold_in(group_key, 1), N_CTX)[:N_CTX // 2]
        source_keys = jax.random.split(jax.random.fold_in(group_key, 2), N_CTX)
        target_keys = jax.random.split(jax.random.fold_in(group_key, 3), N_CTX)
        shuffle = jax.vmap(lambda one_key: jax.random.permutation(one_key, TOK_DEV))(source_keys)
        placing = jax.vmap(lambda one_key: jax.random.permutation(one_key, TOK_DEV))(target_keys)
        sources = jnp.arange(N_CTX, dtype=jnp.int32)[:, None]
        owners = (sources + offsets[shuffle // CAP]) % N_CTX
        local_row = placing[owners, shuffle]
        return (owners * TOK_DEV + local_row).reshape(N_CTX * TOK_DEV).astype(jnp.int32)
    group_keys = jax.vmap(lambda group_index: jax.random.fold_in(key, group_index))(jnp.arange(N_DP))
    return jax.vmap(arrange)(group_keys)


def shard_levels(own_key, extent, cuts, smallest, top_value):
    gain = 1.0
    for dim, blocks in cuts:
        heights = jax.random.uniform(jax.random.fold_in(jax.random.fold_in(own_key, 6), dim), (blocks,), jnp.float32, smallest / len(cuts), top_value / len(cuts))
        gain = gain * jnp.repeat(jnp.exp(heights), extent[dim] // blocks).reshape((-1,) + (1,) * (len(extent) - 1 - dim))
    return gain


def split_up(count, total, reach, slope):
    portions = [(1 << 20) // math.isqrt(standing ** slope) + 1 for standing in range(2, count + 1)]
    surplus, counts = total - reach - (count - 1), [1] * (count - 1)
    while surplus > 0:
        free = [i for i in range(count - 1) if counts[i] < reach]
        whole, left = sum([portions[i] for i in free]), surplus
        for i in free:
            extra = min(reach - counts[i], max(1, left * portions[i] // whole), surplus)
            counts[i] = counts[i] + extra
            surplus = surplus - extra
    return np.array([reach] + counts)


def uneven(rng, amount, total, limit, skew):
    if amount == 2:
        one = jax.random.randint(rng, (), max(1, total - limit), min(limit, total - 1) + 1)
        return jnp.stack([one, total - one])
    sizes = jnp.asarray(split_up(amount, total, limit, skew), jnp.int32)
    twos = (amount - 1) // 2
    source_of, taker = sizes[1:1 + 2 * twos:2], sizes[2:2 + 2 * twos:2]
    margin = jnp.minimum(source_of - 1, limit - taker)
    passed = jax.random.randint(jax.random.fold_in(rng, 1), (twos,), 0, 1 << 20) % (margin + 1)
    sizes = sizes.at[1:1 + 2 * twos:2].set(source_of - passed).at[2:2 + 2 * twos:2].set(taker + passed)
    return sizes[jax.random.permutation(jax.random.fold_in(rng, 2), amount)]


def gaussian(rng, extent, width, limit, cuts=(), held_as=jnp.bfloat16):
    entries = width * jax.random.normal(rng, extent, jnp.float32)
    if cuts:
        entries = entries * shard_levels(rng, extent, cuts, -0.22, 0.18)
    return jnp.clip(entries, -limit, limit).astype(held_as)


def setup_inputs(seed: int = 0) -> dict:
    keys = jax.random.split(jax.random.key(seed), 10)
    return {
        "hidden": gaussian(keys[0], (N_DP, SLAB, D), 1.0, 6.0, ((0, 8), (1, 4))),
        "queries": gaussian(keys[1], (N_DP, SLAB, QH * HD), 1.0, 6.0, ((0, 8), (1, 4))),
        "key_states": gaussian(keys[2], (N_DP, SLAB, KVH * HD), 1.0, 6.0, ((0, 8), (1, 4))),
        "out_grad": gaussian(keys[3], (N_DP, SLAB, QH * HD), 1.0, 6.0, ((0, 8), (1, 4))),
        "w_value": gaussian(keys[4], (D, KVH * HD), D ** -0.5, 0.078125),
        "q_gain": jnp.clip(1.0 + 0.18 * jax.random.normal(keys[5], (HD,), jnp.float32), 0.1, 1.9),
        "k_gain": jnp.clip(1.0 + 0.18 * jax.random.normal(keys[6], (HD,), jnp.float32), 0.1, 1.9),
        "dest_rows": draw_dest_rows(jax.random.fold_in(keys[9], 71), 0),
        "doc_ids": jax.vmap(lambda own: jnp.searchsorted(jnp.cumsum(uneven(own, DOCS, SLAB, DOC_MOST, 2)), jnp.arange(SLAB), side="right"))(jax.random.split(keys[8], N_DP)).reshape((N_DP, SLAB)).astype(jnp.int32),
    }


epsilon = 1e-06
rope_base = 1000000.0
highest = lax.Precision.HIGHEST

def rounded(array):
    return lax.optimization_barrier(array.astype(jnp.bfloat16)).astype(jnp.float32)

def doc_positions(doc_ids):
    position_index = jnp.arange(doc_ids.shape[0], dtype=jnp.int32)
    change = jnp.concatenate([jnp.ones((1,), dtype=bool), doc_ids[1:] != doc_ids[:-1]])
    starts = lax.cummax(jnp.where(change, position_index, 0).astype(jnp.int32), axis=0)
    return position_index - starts

def rope_tables(positions, head_width):
    half_width = head_width // 2
    frequency = rope_base ** (-(jnp.arange(half_width, dtype=jnp.float32) * 2.0 / head_width))
    angles = positions.astype(jnp.float32)[:, None] * frequency[None, :]
    return (jnp.cos(angles), jnp.sin(angles))

def norm_rope(vector, gain_vector, cosine, sine_table):
    inverse_rms = lax.rsqrt(lax.optimization_barrier(jnp.mean(vector * vector, axis=-1, keepdims=True)) + epsilon)
    normed = vector * inverse_rms * gain_vector
    half_width = vector.shape[-1] // 2
    first_half = normed[..., :half_width]
    second_half = normed[..., half_width:]
    cos_rows = cosine[:, None, :]
    sin_rows = sine_table[:, None, :]
    return jnp.concatenate([first_half * cos_rows - second_half * sin_rows, second_half * cos_rows + first_half * sin_rows], axis=-1)

def head_set(q_set, k_head, v_head, g_set, doc_ids, cosine, sine_table, q_gain, k_gain):
    q_normed, q_back = jax.vjp(lambda operand: norm_rope(operand, q_gain, cosine, sine_table), q_set.astype(jnp.float32))
    k_normed, k_back = jax.vjp(lambda operand: norm_rope(operand, k_gain, cosine, sine_table), k_head.astype(jnp.float32))
    q_values = rounded(q_normed)
    k_values = rounded(k_normed)[:, 0]
    v_values = v_head.astype(jnp.float32)
    g_values = g_set.astype(jnp.float32)
    factor = q_set.shape[2] ** (-0.5)
    position_index = jnp.arange(q_set.shape[0], dtype=jnp.int32)
    allowed = (doc_ids[:, None] == doc_ids[None, :]) & (position_index[:, None] >= position_index[None, :])
    logits = jnp.einsum('qhd,kd->hqk', q_values, k_values, precision=highest) * factor
    exponent = jnp.where(allowed[None], jnp.exp(logits), 0.0)
    denominator = lax.optimization_barrier(jnp.sum(exponent, axis=-1))
    outputs = jnp.einsum('hqk,kd->hqd', rounded(exponent), v_values, precision=highest) / denominator[..., None]
    probability = exponent / denominator[..., None]
    delta_row = lax.optimization_barrier(jnp.sum(jnp.swapaxes(g_values, 0, 1) * outputs, axis=-1))
    prob_grad = jnp.einsum('qhd,kd->hqk', g_values, v_values, precision=highest)
    dlogit = rounded(probability * (prob_grad - delta_row[..., None]))
    q_grad = jnp.einsum('hqk,kd->qhd', dlogit, k_values, precision=highest) * factor
    k_grad = jnp.einsum('hqk,qhd->kd', dlogit, q_values, precision=highest) * factor
    v_grad = jnp.einsum('hqk,qhd->kd', rounded(probability), g_values, precision=highest)
    q_pre = q_back(q_grad)[0].astype(jnp.bfloat16)
    k_pre = k_back(k_grad[:, None, :])[0][:, 0].astype(jnp.bfloat16)
    return (q_pre, jnp.concatenate([k_pre, v_grad.astype(jnp.bfloat16)], axis=-1))

def one_group(hidden, queries, key_states, out_grad, dest_rows, doc_ids, w_value, q_gain, k_gain):
    slab_rows = hidden.shape[0]
    head_width = q_gain.shape[0]
    kv_count = key_states.shape[1] // head_width
    set_heads = queries.shape[1] // (N_CTX * head_width)
    share_count = N_CTX // kv_count
    balanced = jnp.zeros_like(hidden).at[dest_rows.astype(jnp.int32)].set(hidden)
    value_rows = jnp.dot(balanced, w_value, preferred_element_type=jnp.float32).astype(jnp.bfloat16)
    cosine, sine_table = rope_tables(doc_positions(doc_ids), head_width)
    q_sets = queries.reshape(slab_rows, N_CTX, set_heads, head_width)
    g_sets = out_grad.reshape(slab_rows, N_CTX, set_heads, head_width)
    k_heads = key_states.reshape(slab_rows, kv_count, head_width)
    v_heads = value_rows.reshape(slab_rows, kv_count, head_width)

    def per_set(set_index):
        head_index = set_index // share_count
        q_set = lax.dynamic_index_in_dim(q_sets, set_index, axis=1, keepdims=False)
        g_set = lax.dynamic_index_in_dim(g_sets, set_index, axis=1, keepdims=False)
        k_head = lax.dynamic_slice_in_dim(k_heads, head_index, 1, axis=1)
        v_head = lax.dynamic_index_in_dim(v_heads, head_index, axis=1, keepdims=False)
        return head_set(q_set, k_head, v_head, g_set, doc_ids, cosine, sine_table, q_gain, k_gain)
    q_parts, kv_parts = lax.map(per_set, jnp.arange(N_CTX, dtype=jnp.int32))
    query_grad = jnp.transpose(q_parts, (1, 0, 2, 3)).reshape(slab_rows, N_CTX * set_heads * head_width)
    summed = kv_parts.astype(jnp.float32).reshape(kv_count, share_count, slab_rows, 2 * head_width).sum(axis=1)
    summed = jnp.transpose(summed, (1, 0, 2))
    key_grad = summed[..., :head_width].astype(jnp.bfloat16).reshape(slab_rows, kv_count * head_width)
    value_grad = summed[..., head_width:].astype(jnp.bfloat16).reshape(slab_rows, kv_count * head_width)
    hidden_grad = jnp.dot(value_grad, w_value.T, preferred_element_type=jnp.float32).astype(jnp.bfloat16)
    weight_part = jnp.dot(balanced.T, value_grad, preferred_element_type=jnp.float32)
    return (hidden_grad, query_grad, key_grad, weight_part)

def reference(hidden, queries, key_states, out_grad, w_value, q_gain, k_gain, dest_rows, doc_ids):

    def accumulate(total, group):
        hidden_grad, query_grad, key_grad, weight_part = one_group(*group, w_value, q_gain, k_gain)
        return (total + weight_part, (hidden_grad, query_grad, key_grad))
    start = jnp.zeros((D, KVH * HD), dtype=jnp.float32)
    total, (hidden_grad, query_grad, key_grad) = lax.scan(accumulate, start, (hidden, queries, key_states, out_grad, dest_rows, doc_ids))
    weight_grad = total / (N_DP * N_CTX)
    return (hidden_grad, query_grad, key_grad, weight_grad)
```

```python
import functools
import math

import jax
import jax.numpy as jnp
import numpy as np
from jax import lax
from jax.experimental import pallas as pl
from jax.experimental.pallas import tpu as pltpu
from jax.sharding import PartitionSpec as P

epsilon = 1e-06
rope_base = 1000000.0
meta_rows = 16
masked = -1e30
VMEM = pltpu.VMEM
f32, bf16 = jnp.float32, jnp.bfloat16
NT = (((1,), (1,)), ((), ()))


def params(mib=48):
    return pltpu.CompilerParams(vmem_limit_bytes=mib << 20)


def cost(flops, bytes_accessed):
    return pl.CostEstimate(flops=int(flops), bytes_accessed=int(bytes_accessed), transcendentals=0)


def rope_constants(rows, blocks, head_width):
    half = head_width // 2
    frequency = rope_base ** (-(np.arange(half) * 2.0 / head_width))
    frequency = np.concatenate([frequency, frequency])
    sign = np.concatenate([-np.ones(half), np.ones(half)])

    def table(positions):
        angles = positions[:, None] * frequency[None, :]
        return np.stack([np.cos(angles), np.sin(angles) * sign]).astype(np.float32)

    return table(np.arange(rows)), table(np.arange(blocks) * rows)


def rotation(rows_ref, base_ref, me):
    cos_b = base_ref[0, pl.ds(me, 1), :]
    sin_b = base_ref[1, pl.ds(me, 1), :]
    cos_r, sin_r = rows_ref[0], rows_ref[1]
    return cos_b * cos_r - sin_b * sin_r, sin_b * cos_r + cos_b * sin_r


def swap_halves(x):
    return pltpu.roll(x, x.shape[-1] // 2, 1)


def norm_rope(u, gain, cosine, sine):
    inverse = lax.rsqrt(jnp.mean(u * u, axis=-1, keepdims=True) + epsilon)
    y = u * inverse * gain
    return y * cosine + swap_halves(y) * sine


def norm_rope_back(u, dz, gain, cosine, sine):
    inverse = lax.rsqrt(jnp.mean(u * u, axis=-1, keepdims=True) + epsilon)
    dn = (dz * cosine + swap_halves(dz * sine)) * gain
    along = jnp.mean(dn * u, axis=-1, keepdims=True) * (inverse * inverse)
    return inverse * (dn - u * along)


def key_message_kernel(k_ref, doc_ref, gain_ref, rows_ref, base_ref, out_ref):
    me = lax.axis_index("ctx")
    rows, width = k_ref.shape
    hd = gain_ref.shape[1]
    cosine, sine = rotation(rows_ref, base_ref, me)
    gain = gain_ref[...]
    marks = jnp.broadcast_to((doc_ref[...] + 1).astype(f32), (meta_rows, rows)).astype(bf16)
    for h in range(width // hd):
        cols = slice(h * hd, (h + 1) * hd)
        u = k_ref[:, cols].astype(f32)
        out_ref[:rows, cols] = norm_rope(u, gain, cosine, sine).astype(bf16)
        out_ref[rows:, cols] = marks


def query_prep_kernel(scale, q_ref, gain_ref, rows_ref, base_ref, out_ref):
    me = lax.axis_index("ctx")
    rows, width = q_ref.shape
    hd = gain_ref.shape[1]
    cosine, sine = rotation(rows_ref, base_ref, me)
    gain = gain_ref[...] * scale
    for h in range(width // hd):
        u = q_ref[:, h * hd : (h + 1) * hd].astype(f32)
        out_ref[0, h * rows : (h + 1) * rows] = norm_rope(u, gain, cosine, sine).astype(bf16)


def value_message_kernel(blocks, h_ref, w_ref, dest_ref, out_ref, acc_ref):
    step = pl.program_id(0)
    rows, width = acc_ref.shape
    part = jnp.dot(h_ref[...], w_ref[...], preferred_element_type=f32)

    @pl.when(step == 0)
    def _():
        acc_ref[...] = part

    @pl.when(step > 0)
    def _():
        acc_ref[...] += part

    @pl.when(step == pl.num_programs(0) - 1)
    def _():
        out_ref[:rows] = acc_ref[...].astype(bf16)
        dest = jnp.broadcast_to(dest_ref[...], (meta_rows, rows))
        block = jnp.zeros_like(dest)
        for j in range(1, blocks):
            block = block + (dest >= j * rows).astype(jnp.int32)
        which = lax.broadcasted_iota(jnp.int32, dest.shape, 0)
        marks = jnp.where(which == 0, block, dest - block * rows).astype(f32).astype(bf16)
        for c in range(width // rows):
            out_ref[rows:, c * rows : (c + 1) * rows] = marks


def share_index(j, half, c, z, core, zs, blocks):
    owner_core = core if half else 1 - core
    return (lax.rem(z + j, zs) * 2 + owner_core) * blocks + c


def feature_kernel(blocks, zs, h_ref, *refs):
    outs, turned = refs[:-1], refs[-1]
    me, dp = lax.axis_index("ctx"), lax.axis_index("dp")
    z, core = dp // 2, dp % 2
    rows, width = h_ref.shape
    share = width // (blocks * zs * 2)
    for c in range(width // 128):
        turned[c * 128 : (c + 1) * 128] = h_ref[:, c * 128 : (c + 1) * 128].T
    for m in range(blocks):
        c = lax.rem(me + m, blocks)
        for half in range(2):
            for j in range(zs):
                start = share_index(j, half, c, z, core, zs, blocks) * share
                start = pl.multiple_of(start, 16)
                at = (half * zs + j) * share
                outs[m][at : at + share] = turned[pl.ds(start, share)]


def mark_rows(ref, rows):
    return ref[rows : rows + meta_rows, :rows].astype(f32)


def attend_kernel(back, qs_ref, g_ref, *refs):
    k_refs = refs[: back + 1]
    p_ref, own_ref = refs[back + 1], refs[back + 2]
    send_refs = refs[back + 3 : 2 * back + 3]
    bias_ref = refs[-1]
    rows = g_ref.shape[0]
    hd = own_ref.shape[1]
    group = g_ref.shape[1] // hd

    @pl.when(pl.program_id(0) == 0)
    def _():
        query_doc = mark_rows(k_refs[0], rows)[:1]
        for b in range(back + 1):
            key_doc = jnp.broadcast_to(mark_rows(k_refs[b], rows)[:1], (rows, rows)).T
            allowed = key_doc == query_doc
            if b == 0:
                key_row = lax.broadcasted_iota(jnp.int32, (rows, rows), 0)
                query_row = lax.broadcasted_iota(jnp.int32, (rows, rows), 1)
                allowed = allowed & (key_row <= query_row)
            bias_ref[b * rows : (b + 1) * rows] = jnp.where(allowed, 0.0, masked)

    keys = jnp.concatenate([r[:rows] for r in k_refs], axis=0)
    logits = lax.dot_general(keys, qs_ref[0], NT, preferred_element_type=f32)
    e = jnp.exp2(logits + jnp.concatenate([bias_ref[...]] * group, axis=1))
    p = (e * (1.0 / jnp.sum(e, axis=0, keepdims=True))).astype(bf16)
    p_ref[0] = p
    g = jnp.concatenate([g_ref[:, j * hd : (j + 1) * hd] for j in range(group)], axis=0)
    gv = jnp.dot(p, g, preferred_element_type=f32)
    own_ref[...] = gv[:rows]
    for b in range(back):
        send_refs[b][...] = gv[(b + 1) * rows : (b + 2) * rows].astype(bf16)


def backward_kernel(back, blocks, factor, p_ref, g_ref, q_ref, qs_ref, gain_ref, rows_ref, base_ref, *refs):
    k_refs, refs = refs[: back + 1], refs[back + 1 :]
    v_refs, refs = refs[:blocks], refs[blocks:]
    gq_ref, own_ref, send_refs, place_ref = refs[0], refs[1], refs[2:-1], refs[-1]
    me = lax.axis_index("ctx")
    rows = g_ref.shape[0]
    hd = own_ref.shape[1]
    group = g_ref.shape[1] // hd
    key_count = (back + 1) * rows

    @pl.when(pl.program_id(0) == 0)
    def _():
        slot = lax.broadcasted_iota(jnp.int32, (key_count, rows), 0).astype(f32)
        for s in range(blocks):
            marks = mark_rows(v_refs[s], rows)
            away = me.astype(f32) - marks[:1]
            away = jnp.where(away < 0, away + blocks, away)
            place_ref[:, s * rows : (s + 1) * rows] = (
                (slot == away * rows + marks[1:2]).astype(f32).astype(bf16)
            )

    arrived = jnp.concatenate([r[:rows] for r in v_refs], axis=0)
    values = jnp.dot(place_ref[...], arrived, preferred_element_type=f32).astype(bf16)
    g = jnp.concatenate([g_ref[:, j * hd : (j + 1) * hd] for j in range(group)], axis=0)
    dp = lax.dot_general(values, g, NT, preferred_element_type=f32)
    p = p_ref[0].astype(f32)
    delta = jnp.sum(p * dp, axis=0, keepdims=True)
    ds = (p * (dp - delta)).astype(bf16)
    gk = jnp.dot(ds, qs_ref[0], preferred_element_type=f32) * math.log(2.0)
    own_ref[...] = gk[:rows]
    for b in range(back):
        send_refs[b][...] = gk[(b + 1) * rows : (b + 2) * rows].astype(bf16)
    keys = jnp.concatenate([r[:rows] for r in k_refs], axis=0)
    gq = jnp.dot(keys.T, ds, preferred_element_type=f32)
    cosine, sine = rotation(rows_ref, base_ref, me)
    gain = gain_ref[...] * factor
    for j in range(group):
        dz = gq[:, j * rows : (j + 1) * rows].T
        u = q_ref[:, j * hd : (j + 1) * hd].astype(f32)
        gq_ref[:, j * hd : (j + 1) * hd] = norm_rope_back(u, dz, gain, cosine, sine).astype(bf16)


def key_back_kernel(k_ref, own_ref, gain_ref, rows_ref, base_ref, *refs):
    got_refs, out_ref = refs[:-1], refs[-1]
    me = lax.axis_index("ctx")
    hd = gain_ref.shape[1]
    cosine, sine = rotation(rows_ref, base_ref, me)
    total = own_ref[...]
    for r in got_refs:
        total = total + r[...].astype(f32)
    for h in range(k_ref.shape[1] // hd):
        cols = slice(h * hd, (h + 1) * hd)
        u = k_ref[:, cols].astype(f32)
        out_ref[:, cols] = norm_rope_back(u, total[:, cols], gain_ref[...], cosine, sine).astype(bf16)


def hidden_grad_kernel(v_ref, w_ref, out_ref):
    out_ref[...] = lax.dot_general(
        v_ref[...], w_ref[...], NT, preferred_element_type=f32
    ).astype(bf16)


def weight_kernel(blocks, *refs):
    h_refs, v_refs, m_refs = refs[:blocks], refs[blocks : 2 * blocks], refs[2 * blocks : 3 * blocks]
    sibling_ref, own_ref = refs[3 * blocks :]
    me = lax.axis_index("ctx")
    rows = h_refs[0].shape[1]
    slab = jnp.concatenate([r[...] for r in v_refs], axis=0)
    slot = lax.broadcasted_iota(jnp.int32, (blocks * rows, rows), 0).astype(f32)
    arrival = []
    for s in range(blocks):
        marks = mark_rows(m_refs[s], rows)
        away = me.astype(f32) - marks[:1]
        away = jnp.where(away < 0, away + blocks, away)
        place = (slot == away * rows + marks[1:2]).astype(f32).T.astype(bf16)
        arrival.append(jnp.dot(place, slab, preferred_element_type=f32).astype(bf16))
    arrival = jnp.concatenate(arrival, axis=0)
    half = sibling_ref.shape[0]
    features = jnp.concatenate([r[...] for r in h_refs], axis=1)
    sibling_ref[...] = jnp.dot(features[:half], arrival, preferred_element_type=f32).astype(bf16)
    own_ref[...] = jnp.dot(features[half:], arrival, preferred_element_type=f32)


def on_device(hidden, queries, key_states, out_grad, w_value, q_gain, k_gain, dest_rows, doc_ids):
    hidden, queries, key_states, out_grad = hidden[0], queries[0], key_states[0], out_grad[0]
    rows, width = hidden.shape
    hd = q_gain.shape[0]
    kv_width = key_states.shape[1]
    q_width = queries.shape[1]
    kv = kv_width // hd
    group = q_width // kv_width
    blocks, dp_count = lax.axis_size("ctx"), lax.axis_size("dp")
    zs = dp_count // 2
    back = blocks // 2
    factor = hd ** (-0.5)
    share = width // (blocks * dp_count)
    spread = group * rows
    key_count = (back + 1) * rows
    message = jax.ShapeDtypeStruct((rows + meta_rows, kv_width), bf16)
    rows_table, base_table = (jnp.asarray(t) for t in rope_constants(rows, blocks, hd))
    q_gain, k_gain = q_gain[None], k_gain[None]

    def ahead(array, m):
        return lax.ppermute(array, "ctx", [(i, i + m) for i in range(blocks - m)])

    def behind(array, m):
        return lax.ppermute(array, "ctx", [(i + m, i) for i in range(blocks - m)])

    def around(array, m):
        return lax.ppermute(array, "ctx", [(i, (i + m) % blocks) for i in range(blocks)])

    def call(kernel, out_shape, name, flops=0, nbytes=0, **kw):
        return pl.pallas_call(
            kernel, out_shape=out_shape, name=name, compiler_params=params(),
            cost_estimate=cost(flops, nbytes), **kw,
        )

    def whole(shape):
        return pl.BlockSpec(shape, lambda h: (0,) * len(shape))

    key_own = call(key_message_kernel, message, "key_message", 0, 1e6)(
        key_states, doc_ids, k_gain, rows_table, base_table
    )
    key_messages = [key_own] + [ahead(key_own, m) for m in range(1, back + 1)]

    head_cols = pl.BlockSpec((rows, group * hd), lambda h: (0, h))
    head_set = pl.BlockSpec((1, spread, hd), lambda h: (h, 0, 0))
    message_cols = pl.BlockSpec((rows + meta_rows, hd), lambda h: (0, h))
    row_cols = pl.BlockSpec((rows, hd), lambda h: (0, h))
    tables = [whole((1, hd)), whole(rows_table.shape), whole(base_table.shape)]

    q_scaled = call(
        functools.partial(query_prep_kernel, factor * math.log2(math.e)),
        jax.ShapeDtypeStruct((kv, spread, hd), bf16),
        "query_prep", 0, 4e6, grid=(kv,), in_specs=[head_cols] + tables, out_specs=head_set,
    )(queries, q_gain, rows_table, base_table)

    depth = width // 4
    value_own = call(
        functools.partial(value_message_kernel, blocks),
        message, "value_message", 2 * rows * width * kv_width, 7e6, grid=(width // depth,),
        in_specs=[
            pl.BlockSpec((rows, depth), lambda i: (0, i)),
            pl.BlockSpec((depth, kv_width), lambda i: (i, 0)),
            whole((1, rows)),
        ],
        out_specs=whole((rows + meta_rows, kv_width)),
        scratch_shapes=[VMEM((rows, kv_width), f32)],
    )(hidden, w_value, dest_rows)
    value_messages = [value_own] + [around(value_own, m) for m in range(1, blocks)]

    if share % 16 == 0:
        features = call(
            functools.partial(feature_kernel, blocks, zs),
            [jax.ShapeDtypeStruct((width // blocks, rows), bf16)] * blocks,
            "features", 0, 6e6, scratch_shapes=[VMEM((width, rows), bf16)],
        )(hidden)
    else:
        me, dp = lax.axis_index("ctx"), lax.axis_index("dp")
        turned = hidden.T.reshape(dp_count * blocks, share, rows)
        features = []
        for m in range(blocks):
            places = [
                share_index(j, half, lax.rem(me + m, blocks), dp // 2, dp % 2, zs, blocks)
                for half in range(2)
                for j in range(zs)
            ]
            pieces = [lax.dynamic_index_in_dim(turned, place, axis=0) for place in places]
            features.append(jnp.concatenate(pieces, axis=0).reshape(width // blocks, rows))
    features = [features[0]] + [around(features[m], m) for m in range(1, blocks)]

    attended = call(
        functools.partial(attend_kernel, back),
        [
            jax.ShapeDtypeStruct((kv, key_count, spread), bf16),
            jax.ShapeDtypeStruct((rows, kv_width), f32),
        ]
        + [jax.ShapeDtypeStruct((rows, kv_width), bf16)] * back,
        "attend", 8 * kv * key_count * spread * hd, 5e6, grid=(kv,),
        in_specs=[head_set, head_cols] + [message_cols] * (back + 1),
        out_specs=[pl.BlockSpec((1, key_count, spread), lambda h: (h, 0, 0))]
        + [row_cols] * (back + 1),
        scratch_shapes=[VMEM((key_count, rows), f32)],
    )(q_scaled, out_grad, *key_messages)
    probabilities, value_total = attended[0], attended[1]
    for m in range(1, back + 1):
        value_total = value_total + behind(attended[1 + m], m).astype(f32)
    value_grad = value_total.astype(bf16)
    value_grads = [value_grad] + [around(value_grad, m) for m in range(1, blocks)]

    backed = call(
        functools.partial(backward_kernel, back, blocks, factor),
        [
            jax.ShapeDtypeStruct((rows, q_width), bf16),
            jax.ShapeDtypeStruct((rows, kv_width), f32),
        ]
        + [jax.ShapeDtypeStruct((rows, kv_width), bf16)] * back,
        "backward", 12 * kv * key_count * spread * hd, 7e6, grid=(kv,),
        in_specs=[
            pl.BlockSpec((1, key_count, spread), lambda h: (h, 0, 0)),
            head_cols, head_cols, head_set,
        ]
        + tables + [message_cols] * (back + 1 + blocks),
        out_specs=[head_cols] + [row_cols] * (back + 1),
        scratch_shapes=[VMEM((key_count, blocks * rows), bf16)],
    )(
        probabilities, out_grad, queries, q_scaled, q_gain, rows_table, base_table,
        *key_messages, *value_messages,
    )
    query_grad = backed[0]
    key_got = [behind(backed[1 + m], m) for m in range(1, back + 1)]
    key_grad = call(
        key_back_kernel, jax.ShapeDtypeStruct((rows, kv_width), bf16), "key_back", 0, 1e6
    )(key_states, backed[1], k_gain, rows_table, base_table, *key_got)

    slice_width = width // 4
    hidden_grad = call(
        hidden_grad_kernel, jax.ShapeDtypeStruct((rows, width), bf16),
        "hidden_grad", 2 * rows * width * kv_width, 7e6, grid=(width // slice_width,),
        in_specs=[whole((rows, kv_width)), pl.BlockSpec((slice_width, kv_width), lambda i: (i, 0))],
        out_specs=pl.BlockSpec((rows, slice_width), lambda i: (0, i)),
    )(value_grad, w_value)

    half = width // blocks // 2
    sibling, own = call(
        functools.partial(weight_kernel, blocks),
        [jax.ShapeDtypeStruct((half, kv_width), bf16), jax.ShapeDtypeStruct((half, kv_width), f32)],
        "weight", 2 * width * rows * kv_width, 4e6,
    )(*features, *value_grads, *value_messages)
    got = lax.ppermute(sibling, "dp", [(d, d ^ 1) for d in range(dp_count)])
    pair = own.reshape(zs, share, kv_width) + got.astype(f32).reshape(zs, share, kv_width)
    total = pair[0]
    for j in range(1, zs):
        route = [(z * 2 + c, (z + j) % zs * 2 + c) for z in range(zs) for c in range(2)]
        total = total + lax.ppermute(pair[j].astype(bf16), "dp", route).astype(f32)
    weight_grad = total * (1.0 / (blocks * dp_count))
    return (hidden_grad[None], query_grad[None], key_grad[None], weight_grad)


def solution(mesh):
    return jax.shard_map(
        on_device,
        mesh=mesh,
        in_specs=(
            P("dp", "ctx", None),
            P("dp", "ctx", None),
            P("dp", "ctx", None),
            P("dp", "ctx", None),
            P(),
            P(),
            P(),
            P("dp", "ctx"),
            P("dp", "ctx"),
        ),
        out_specs=(
            P("dp", "ctx", None),
            P("dp", "ctx", None),
            P("dp", "ctx", None),
            P(("dp", "ctx"), None),
        ),
        check_vma=False,
    )
```

```python
import functools
import math

import jax
import jax.numpy as jnp
import numpy as np
from jax import lax
from jax.experimental import pallas as pl
from jax.experimental.pallas import tpu as pltpu
from jax.sharding import PartitionSpec as P

epsilon = 1e-06
rope_base = 1000000.0
meta_rows = 16
masked = -1e30
VMEM = pltpu.VMEM
f32, bf16 = jnp.float32, jnp.bfloat16
NT = (((1,), (1,)), ((), ()))


def params(mib):
    return pltpu.CompilerParams(vmem_limit_bytes=mib << 20)


def ordered(kernel, inputs, after):
    def body(*refs):
        kernel(*refs[:inputs], *refs[inputs + after :])

    return body


def cost(flops, bytes_accessed):
    return pl.CostEstimate(flops=int(flops), bytes_accessed=int(bytes_accessed), transcendentals=0)


def rope_constants(rows, blocks, head_width):
    half = head_width // 2
    frequency = rope_base ** (-(np.arange(half) * 2.0 / head_width))
    frequency = np.concatenate([frequency, frequency])
    sign = np.concatenate([-np.ones(half), np.ones(half)])

    def table(positions):
        angles = positions[:, None] * frequency[None, :]
        return np.stack([np.cos(angles), np.sin(angles) * sign]).astype(np.float32)

    return table(np.arange(rows)), table(np.arange(blocks) * rows)


def rotation(rows_ref, base_ref, me):
    cos_b = base_ref[0, pl.ds(me, 1), :]
    sin_b = base_ref[1, pl.ds(me, 1), :]
    cos_r, sin_r = rows_ref[0], rows_ref[1]
    return cos_b * cos_r - sin_b * sin_r, sin_b * cos_r + cos_b * sin_r


def swap_halves(x):
    return pltpu.roll(x, x.shape[-1] // 2, 1)


def norm_rope(u, gain, cosine, sine):
    inverse = lax.rsqrt(jnp.mean(u * u, axis=-1, keepdims=True) + epsilon)
    y = u * inverse * gain
    return y * cosine + swap_halves(y) * sine


def norm_rope_back(u, dz, gain, cosine, sine):
    inverse = lax.rsqrt(jnp.mean(u * u, axis=-1, keepdims=True) + epsilon)
    dn = (dz * cosine + swap_halves(dz * sine)) * gain
    along = jnp.mean(dn * u, axis=-1, keepdims=True) * (inverse * inverse)
    return inverse * (dn - u * along)


def message_kernel(blocks, *refs):
    sources, (out_ref, far_ref, *held, sems) = refs[:8], refs[8:]
    me = lax.axis_index("ctx")
    w_held, h_held = held[-1], held[-2]
    rows, width = h_held.shape
    parts = 8
    part = width // parts
    copies = [pltpu.make_async_copy(a, b, sems.at[i]) for i, (a, b) in enumerate(zip(sources[:7], held))]
    for i in range(parts):
        piece = pl.ds(i * part, part)
        copies.append(
            pltpu.make_async_copy(sources[7].at[piece], w_held.at[piece], sems.at[7 + i])
        )
    for copy in copies:
        copy.start()
    for copy in copies[:6]:
        copy.wait()
    k_ref, doc_ref, dest_ref, gain_ref, rows_ref, base_ref = held[:6]
    kv_width = k_ref.shape[1]
    hd = gain_ref.shape[1]
    cosine, sine = rotation(rows_ref, base_ref, me)
    dest = jnp.broadcast_to(dest_ref[...], (meta_rows, rows))
    block = jnp.zeros_like(dest)
    for j in range(1, blocks):
        block = block + (dest >= j * rows).astype(jnp.int32)
    which = lax.broadcasted_iota(jnp.int32, dest.shape, 0)
    marks = jnp.where(which == 0, block, dest - block * rows)
    marks = jnp.where(which == 2, doc_ref[...] + 1, marks).astype(f32).astype(bf16)
    for h in range(kv_width // hd):
        cols = slice(h * hd, (h + 1) * hd)
        u = k_ref[:, cols].astype(f32)
        out_ref[rows + meta_rows :, cols] = norm_rope(u, gain_ref[...], cosine, sine).astype(bf16)
        out_ref[rows : rows + meta_rows, cols] = marks
        far_ref[rows:, cols] = marks
    copies[6].wait()
    total = None
    for i in range(parts):
        copies[7 + i].wait()
        piece = slice(i * part, (i + 1) * part)
        product = jnp.dot(h_held[:, piece], w_held[piece], preferred_element_type=f32)
        total = product if total is None else total + product
    out_ref[:rows] = total.astype(bf16)
    far_ref[:rows] = total.astype(bf16)


def upright_tables(gain_ref, rows_ref, base_ref, scale, held):
    rows = rows_ref.shape[1]
    cosine, sine = rotation(rows_ref, base_ref, lax.axis_index("ctx"))
    held[0] = cosine.T
    held[1] = sine.T
    held[2] = jnp.broadcast_to(gain_ref[...] * scale, (rows, gain_ref.shape[1])).T


def swap_rows(x):
    half = x.shape[0] // 2
    return jnp.concatenate([x[half:], x[:half]], axis=0)


def query_prep_kernel(scale, q_ref, gain_ref, rows_ref, base_ref, scaled_ref, turned_ref, held):
    rows, width = q_ref.shape
    hd = gain_ref.shape[1]

    @pl.when(pl.program_id(0) == 0)
    def _():
        upright_tables(gain_ref, rows_ref, base_ref, scale, held)

    for h in range(width // hd):
        turned = q_ref[:, h * hd : (h + 1) * hd].T
        turned_ref[0, :, h * rows : (h + 1) * rows] = turned
        u = turned.astype(f32)
        inverse = lax.rsqrt(jnp.mean(u * u, axis=0, keepdims=True) + epsilon)
        y = u * inverse * held[2]
        z = y * held[0] + swap_rows(y) * held[1]
        scaled_ref[0, :, h * rows : (h + 1) * rows] = z.astype(bf16)


def share_index(j, half, c, z, core, zs, blocks):
    owner_core = core if half else 1 - core
    return ((z ^ j) * 2 + owner_core) * blocks + c


def feature_kernel(blocks, zs, h_hbm, *refs):
    outs, (held, turned, sems) = refs[:blocks], refs[blocks:]
    me, dp = lax.axis_index("ctx"), lax.axis_index("dp")
    z, core = dp // 2, dp % 2
    parts, rows, part = held.shape
    share = turned.shape[0] // (blocks * zs * 2)
    copies = [
        pltpu.make_async_copy(h_hbm.at[:, i * part : (i + 1) * part], held.at[i], sems.at[i])
        for i in range(parts)
    ]
    for copy in copies:
        copy.start()
    for i, copy in enumerate(copies):
        copy.wait()
        for c in range(part // 128):
            at = i * part + c * 128
            turned[at : at + 128] = held[i, :, c * 128 : (c + 1) * 128].T
    for m in range(blocks):
        c = lax.rem(me + m, blocks)
        for half in range(2):
            for j in range(zs):
                start = share_index(j, half, c, z, core, zs, blocks) * share
                start = pl.multiple_of(start, 16)
                at = (half * zs + j) * share
                outs[m][at : at + share] = turned[pl.ds(start, share)]


def mark_rows(ref, rows):
    return ref[rows : rows + meta_rows, :rows].astype(f32)


def attend_kernel(back, qs_ref, g_ref, *refs):
    k_refs = refs[: back + 1]
    p_ref, own_ref = refs[back + 1], refs[back + 2]
    send_refs = refs[back + 3 : 2 * back + 3]
    bias_ref = refs[-1]
    rows = g_ref.shape[0]
    hd = own_ref.shape[1]
    group = g_ref.shape[1] // hd

    @pl.when(pl.program_id(0) == 0)
    def _():
        query_doc = mark_rows(k_refs[0], rows)[2:3]
        for b in range(back + 1):
            key_doc = jnp.broadcast_to(mark_rows(k_refs[b], rows)[2:3], (rows, rows)).T
            allowed = key_doc == query_doc
            if b == 0:
                key_row = lax.broadcasted_iota(jnp.int32, (rows, rows), 0)
                query_row = lax.broadcasted_iota(jnp.int32, (rows, rows), 1)
                allowed = allowed & (key_row <= query_row)
            else:
                allowed = allowed & (lax.axis_index("ctx") >= b)
            bias_ref[b * rows : (b + 1) * rows] = jnp.where(allowed, 0.0, masked)

    keys = jnp.concatenate([r[rows + meta_rows :] for r in k_refs], axis=0)
    logits = jnp.dot(keys, qs_ref[0], preferred_element_type=f32)
    e = jnp.exp2(logits + jnp.concatenate([bias_ref[...]] * group, axis=1))
    p = (e * (1.0 / jnp.sum(e, axis=0, keepdims=True))).astype(bf16)
    p_ref[0] = p
    g = jnp.concatenate([g_ref[:, j * hd : (j + 1) * hd] for j in range(group)], axis=0)
    gv = jnp.dot(p, g, preferred_element_type=f32)
    own_ref[...] = gv[:rows]
    for b in range(back):
        send_refs[b][...] = gv[(b + 1) * rows : (b + 2) * rows].astype(bf16)


def backward_kernel(back, blocks, factor, p_ref, g_ref, u_ref, qs_ref, gain_ref, rows_ref, base_ref, *refs):
    v_refs, refs = refs[:blocks], refs[blocks:]
    k_refs = v_refs[: back + 1]
    gq_ref, own_ref, send_refs, place_ref, held = refs[0], refs[1], refs[2:-2], refs[-2], refs[-1]
    me = lax.axis_index("ctx")
    rows = g_ref.shape[0]
    hd = own_ref.shape[1]
    group = g_ref.shape[1] // hd
    key_count = (back + 1) * rows

    @pl.when(pl.program_id(0) == 0)
    def _():
        upright_tables(gain_ref, rows_ref, base_ref, factor, held)
        slot = lax.broadcasted_iota(jnp.int32, (key_count, rows), 0).astype(f32)
        for s in range(blocks):
            marks = mark_rows(v_refs[s], rows)
            away = me.astype(f32) - marks[:1]
            away = jnp.where(away < 0, away + blocks, away)
            place_ref[:, s * rows : (s + 1) * rows] = (
                (slot == away * rows + marks[1:2]).astype(f32).astype(bf16)
            )

    arrived = jnp.concatenate([r[:rows] for r in v_refs], axis=0)
    values = jnp.dot(place_ref[...], arrived, preferred_element_type=f32).astype(bf16)
    g = jnp.concatenate([g_ref[:, j * hd : (j + 1) * hd] for j in range(group)], axis=0)
    dp = lax.dot_general(values, g, NT, preferred_element_type=f32)
    p = p_ref[0].astype(f32)
    delta = jnp.sum(p * dp, axis=0, keepdims=True)
    ds = (p * (dp - delta)).astype(bf16)
    gk = lax.dot_general(ds, qs_ref[0], NT, preferred_element_type=f32) * math.log(2.0)
    own_ref[...] = gk[:rows]
    for b in range(back):
        send_refs[b][...] = gk[(b + 1) * rows : (b + 2) * rows].astype(bf16)
    keys = jnp.concatenate([r[rows + meta_rows :] for r in k_refs], axis=0)
    gq = jnp.dot(keys.T, ds, preferred_element_type=f32)
    for j in range(group):
        cols = slice(j * rows, (j + 1) * rows)
        dz, u = gq[:, cols], u_ref[0, :, cols].astype(f32)
        inverse = lax.rsqrt(jnp.mean(u * u, axis=0, keepdims=True) + epsilon)
        dn = (dz * held[0] + swap_rows(dz * held[1])) * held[2]
        along = jnp.mean(dn * u, axis=0, keepdims=True) * (inverse * inverse)
        gq_ref[:, j * hd : (j + 1) * hd] = (inverse * (dn - u * along)).astype(bf16).T


def key_back_kernel(k_ref, own_ref, gain_ref, rows_ref, base_ref, *refs):
    got_refs, out_ref = refs[:-1], refs[-1]
    me = lax.axis_index("ctx")
    hd = gain_ref.shape[1]
    cosine, sine = rotation(rows_ref, base_ref, me)
    total = own_ref[...]
    for r in got_refs:
        total = total + r[...].astype(f32)
    for h in range(k_ref.shape[1] // hd):
        cols = slice(h * hd, (h + 1) * hd)
        u = k_ref[:, cols].astype(f32)
        out_ref[:, cols] = norm_rope_back(u, total[:, cols], gain_ref[...], cosine, sine).astype(bf16)


def gate_kernel(*refs):
    pass


def value_sum_kernel(*refs):
    total = refs[0][...]
    for r in refs[1:-1]:
        total = total + r[...].astype(f32)
    refs[-1][...] = total.astype(bf16)


def pair_kernel(own_ref, got_ref, first_ref, *send_refs):
    share = first_ref.shape[0]
    first_ref[...] = own_ref[:share] + got_ref[:share].astype(f32)
    for j, ref in enumerate(send_refs, 1):
        at = slice(j * share, (j + 1) * share)
        ref[...] = (own_ref[at] + got_ref[at].astype(f32)).astype(bf16)


def total_kernel(first_ref, *refs):
    total = first_ref[...]
    for r in refs[:-1]:
        total = total + r[...].astype(f32)
    refs[-1][...] = total * (1.0 / (lax.axis_size("ctx") * lax.axis_size("dp")))


def hidden_grad_kernel(v_ref, w_ref, out_ref):
    out_ref[...] = lax.dot_general(
        v_ref[...], w_ref[...], NT, preferred_element_type=f32
    ).astype(bf16)


def weight_kernel(blocks, *refs):
    h_refs, slab_ref, m_refs = refs[:blocks], refs[blocks], refs[blocks + 1 : 2 * blocks + 1]
    sibling_ref, own_ref = refs[2 * blocks + 1 :]
    rows = h_refs[0].shape[1]
    slot = lax.broadcasted_iota(jnp.int32, (blocks * rows, rows), 0).astype(f32)
    arrival = []
    for s in range(blocks):
        marks = mark_rows(m_refs[s], rows)
        place = (slot == marks[:1] * rows + marks[1:2]).astype(f32).T.astype(bf16)
        arrival.append(jnp.dot(place, slab_ref[...], preferred_element_type=f32).astype(bf16))
    arrival = jnp.concatenate(arrival, axis=0)
    half = sibling_ref.shape[0]
    features = jnp.concatenate([r[...] for r in h_refs], axis=1)
    sibling_ref[...] = jnp.dot(features[:half], arrival, preferred_element_type=f32).astype(bf16)
    own_ref[...] = jnp.dot(features[half:], arrival, preferred_element_type=f32)


def on_device(hidden, queries, key_states, out_grad, w_value, q_gain, k_gain, dest_rows, doc_ids):
    hidden, queries, key_states, out_grad = hidden[0], queries[0], key_states[0], out_grad[0]
    rows, width = hidden.shape
    hd = q_gain.shape[0]
    kv_width = key_states.shape[1]
    q_width = queries.shape[1]
    kv = kv_width // hd
    group = q_width // kv_width
    blocks, dp_count = lax.axis_size("ctx"), lax.axis_size("dp")
    zs = dp_count // 2
    back = blocks // 2
    factor = hd ** (-0.5)
    share = width // (blocks * dp_count)
    spread = group * rows
    key_count = (back + 1) * rows
    message = jax.ShapeDtypeStruct((2 * rows + meta_rows, kv_width), bf16)
    far_message = jax.ShapeDtypeStruct((rows + meta_rows, kv_width), bf16)
    rows_table, base_table = (jnp.asarray(t) for t in rope_constants(rows, blocks, hd))
    q_gain, k_gain = q_gain[None], k_gain[None]

    def behind(array, m):
        return lax.ppermute(array, "ctx", [(i + m, i) for i in range(blocks - m)])

    def around(array, m):
        return lax.ppermute(array, "ctx", [(i, (i + m) % blocks) for i in range(blocks)])

    def call(kernel, out_shape, name, operands, mib, flops=0, nbytes=0, in_specs=None, after=(), **kw):
        if in_specs is None:
            in_specs = [pl.BlockSpec(memory_space=VMEM)] * len(operands)
        return pl.pallas_call(
            ordered(kernel, len(operands), len(after)), out_shape=out_shape, name=name,
            compiler_params=params(mib), cost_estimate=cost(flops, nbytes),
            in_specs=list(in_specs) + [pl.BlockSpec(memory_space=pl.ANY)] * len(after), **kw,
        )(*operands, *after)

    def in_hbm(array):
        return pltpu.with_memory_space_constraint(array, pltpu.HBM)

    def gate(arrays, after, name):
        return pl.pallas_call(
            gate_kernel, name=name, compiler_params=params(1), cost_estimate=cost(0, 0),
            out_shape=[jax.ShapeDtypeStruct(a.shape, a.dtype) for a in arrays],
            in_specs=[pl.BlockSpec(memory_space=pl.ANY)] * (len(arrays) + len(after)),
            out_specs=[pl.BlockSpec(memory_space=pl.ANY)] * len(arrays),
            input_output_aliases={i: i for i in range(len(arrays))},
        )(*arrays, *after)

    def whole(shape):
        return pl.BlockSpec(shape, lambda h: (0,) * len(shape))

    sources = [in_hbm(a) for a in (key_states, doc_ids, dest_rows, k_gain, rows_table, base_table, hidden, w_value)]
    message_own, message_far = call(
        functools.partial(message_kernel, blocks), [message, far_message], "message", sources, 16,
        2 * rows * width * kv_width, 7e6,
        in_specs=[pl.BlockSpec(memory_space=pltpu.HBM)] * 8,
        scratch_shapes=[VMEM(a.shape, a.dtype) for a in sources] + [pltpu.SemaphoreType.DMA((15,))],
    )
    messages = [message_own]
    messages += [around(message_own if m <= back else message_far, m) for m in range(1, blocks)]

    head_cols = pl.BlockSpec((rows, group * hd), lambda h: (0, h))
    head_set = pl.BlockSpec((1, hd, spread), lambda h: (h, 0, 0))
    message_cols = pl.BlockSpec((2 * rows + meta_rows, hd), lambda h: (0, h))
    far_cols = pl.BlockSpec((rows + meta_rows, hd), lambda h: (0, h))
    row_cols = pl.BlockSpec((rows, hd), lambda h: (0, h))
    table_specs = [whole((1, hd)), whole(rows_table.shape), whole(base_table.shape)]
    upright = VMEM((3, hd, rows), f32)

    q_scaled, q_turned = call(
        functools.partial(query_prep_kernel, factor * math.log2(math.e)),
        [jax.ShapeDtypeStruct((kv, hd, spread), bf16)] * 2,
        "query_prep", (queries, q_gain, rows_table, base_table), 8, 0, 4e6, grid=(kv,),
        in_specs=[head_cols] + table_specs, out_specs=[head_set] * 2, scratch_shapes=[upright],
        after=(message_own,),
    )

    if share % 16 == 0:
        features = call(
            functools.partial(feature_kernel, blocks, zs),
            [jax.ShapeDtypeStruct((width // blocks, rows), bf16)] * blocks,
            "features", (in_hbm(hidden),), 8, 0, 6e6,
            in_specs=[pl.BlockSpec(memory_space=pltpu.HBM)], after=(q_scaled,),
            scratch_shapes=[
                VMEM((4, rows, width // 4), bf16),
                VMEM((width, rows), bf16),
                pltpu.SemaphoreType.DMA((4,)),
            ],
        )
    else:
        me, dp = lax.axis_index("ctx"), lax.axis_index("dp")
        turned = hidden.T.reshape(dp_count * blocks, share, rows)
        features = []
        for m in range(blocks):
            places = [
                share_index(j, half, lax.rem(me + m, blocks), dp // 2, dp % 2, zs, blocks)
                for half in range(2)
                for j in range(zs)
            ]
            pieces = [lax.dynamic_index_in_dim(turned, place, axis=0) for place in places]
            features.append(jnp.concatenate(pieces, axis=0).reshape(width // blocks, rows))
    first_features = features[0]
    leaving = gate(features[1:], messages[1 : back + 1], "features_leave")
    features = [first_features] + [around(leaving[m - 1], m) for m in range(1, blocks)]

    attended = call(
        functools.partial(attend_kernel, back),
        [
            jax.ShapeDtypeStruct((kv, key_count, spread), bf16),
            jax.ShapeDtypeStruct((rows, kv_width), f32),
        ]
        + [jax.ShapeDtypeStruct((rows, kv_width), bf16)] * back,
        "attend", (q_scaled, out_grad, *messages[: back + 1]), 16,
        8 * kv * key_count * spread * hd, 5e6, grid=(kv,),
        in_specs=[head_set, head_cols] + [message_cols] * (back + 1),
        out_specs=[pl.BlockSpec((1, key_count, spread), lambda h: (h, 0, 0))]
        + [row_cols] * (back + 1),
        scratch_shapes=[VMEM((key_count, rows), f32)], after=(leaving[0],),
    )
    probabilities, value_total = attended[0], attended[1]
    value_got = [behind(attended[1 + m], m) for m in range(1, back + 1)]

    backed = call(
        functools.partial(backward_kernel, back, blocks, factor),
        [
            jax.ShapeDtypeStruct((rows, q_width), bf16),
            jax.ShapeDtypeStruct((rows, kv_width), f32),
        ]
        + [jax.ShapeDtypeStruct((rows, kv_width), bf16)] * back,
        "backward",
        (
            probabilities, out_grad, q_turned, q_scaled, q_gain, rows_table, base_table,
            *messages,
        ),
        20, 12 * kv * key_count * spread * hd, 7e6, grid=(kv,),
        in_specs=[
            pl.BlockSpec((1, key_count, spread), lambda h: (h, 0, 0)),
            head_cols, head_set, head_set,
        ]
        + table_specs + [message_cols] * (back + 1) + [far_cols] * (blocks - back - 1),
        out_specs=[head_cols] + [row_cols] * (back + 1),
        scratch_shapes=[VMEM((key_count, blocks * rows), bf16), upright],
        after=(value_total,),
    )
    value_grad = call(
        value_sum_kernel, jax.ShapeDtypeStruct((rows, kv_width), bf16), "value_sum",
        (value_total, *value_got), 4, 0, 1e6, after=(backed[1], *features[1:]),
    )
    slab_value_grad = lax.all_gather(value_grad, "ctx", axis=0, tiled=True)

    half = width // blocks // 2
    sibling, own = call(
        functools.partial(weight_kernel, blocks),
        [jax.ShapeDtypeStruct((half, kv_width), bf16), jax.ShapeDtypeStruct((half, kv_width), f32)],
        "weight", (*features, slab_value_grad, *messages), 16, 2 * width * rows * kv_width, 4e6,
    )
    got = lax.ppermute(sibling, "dp", [(d, d ^ 1) for d in range(dp_count)])

    slice_width = width // 4
    hidden_grad = call(
        hidden_grad_kernel, jax.ShapeDtypeStruct((rows, width), bf16),
        "hidden_grad", (value_grad, w_value), 8, 2 * rows * width * kv_width, 7e6,
        grid=(width // slice_width,),
        in_specs=[whole((rows, kv_width)), pl.BlockSpec((slice_width, kv_width), lambda i: (i, 0))],
        out_specs=pl.BlockSpec((rows, slice_width), lambda i: (0, i)),
        after=(),
    )

    pairs = call(
        pair_kernel,
        [jax.ShapeDtypeStruct((share, kv_width), f32)]
        + [jax.ShapeDtypeStruct((share, kv_width), bf16)] * (zs - 1),
        "pair", (own, got), 12, 0, 3e6,
    )
    sums = []
    for j in range(1, zs):
        route = [(z * 2 + c, (z ^ j) * 2 + c) for z in range(zs) for c in range(2)]
        sums.append(lax.ppermute(pairs[j], "dp", route))

    query_grad = backed[0]
    key_leaving = gate(backed[2:], (pairs[0],), "keys_leave")
    key_got = [behind(key_leaving[m - 1], m) for m in range(1, back + 1)]
    weight_grad = call(
        total_kernel, jax.ShapeDtypeStruct((share, kv_width), f32), "total",
        (pairs[0], *sums), 4, 0, 1e6,
    )
    key_grad = call(
        key_back_kernel, jax.ShapeDtypeStruct((rows, kv_width), bf16), "key_back",
        (key_states, backed[1], k_gain, rows_table, base_table, *key_got), 4, 0, 1e6,
    )
    return (hidden_grad[None], query_grad[None], key_grad[None], weight_grad)


def solution(mesh):
    return jax.shard_map(
        on_device,
        mesh=mesh,
        in_specs=(
            P("dp", "ctx", None),
            P("dp", "ctx", None),
            P("dp", "ctx", None),
            P("dp", "ctx", None),
            P(),
            P(),
            P(),
            P("dp", "ctx"),
            P("dp", "ctx"),
        ),
        out_specs=(
            P("dp", "ctx", None),
            P("dp", "ctx", None),
            P("dp", "ctx", None),
            P(("dp", "ctx"), None),
        ),
        check_vma=False,
    )
```

```python
import functools
import math

import jax
import jax.numpy as jnp
import numpy as np
from jax import lax
from jax.experimental import pallas as pl
from jax.experimental.pallas import tpu as pltpu
from jax.sharding import PartitionSpec as P

epsilon = 1e-06
rope_base = 1000000.0
meta_rows = 16
masked = -1e30
VMEM = pltpu.VMEM
f32, bf16 = jnp.float32, jnp.bfloat16
NT = (((1,), (1,)), ((), ()))


def params(mib):
    return pltpu.CompilerParams(vmem_limit_bytes=mib << 20)


def ordered(kernel, inputs, after):
    def body(*refs):
        kernel(*refs[:inputs], *refs[inputs + after :])

    return body


def cost(flops, bytes_accessed):
    return pl.CostEstimate(flops=int(flops), bytes_accessed=int(bytes_accessed), transcendentals=0)


def rope_constants(rows, blocks, head_width):
    half = head_width // 2
    frequency = rope_base ** (-(np.arange(half) * 2.0 / head_width))
    frequency = np.concatenate([frequency, frequency])
    sign = np.concatenate([-np.ones(half), np.ones(half)])

    def table(positions):
        angles = positions[:, None] * frequency[None, :]
        return np.stack([np.cos(angles), np.sin(angles) * sign]).astype(np.float32)

    return table(np.arange(rows)), table(np.arange(blocks) * rows)


def rotation(rows_ref, base_ref, me):
    cos_b = base_ref[0, pl.ds(me, 1), :]
    sin_b = base_ref[1, pl.ds(me, 1), :]
    cos_r, sin_r = rows_ref[0], rows_ref[1]
    return cos_b * cos_r - sin_b * sin_r, sin_b * cos_r + cos_b * sin_r


def swap_halves(x):
    return pltpu.roll(x, x.shape[-1] // 2, 1)


def norm_rope(u, gain, cosine, sine):
    inverse = lax.rsqrt(jnp.mean(u * u, axis=-1, keepdims=True) + epsilon)
    y = u * inverse * gain
    return y * cosine + swap_halves(y) * sine


def norm_rope_back(u, dz, gain, cosine, sine):
    inverse = lax.rsqrt(jnp.mean(u * u, axis=-1, keepdims=True) + epsilon)
    dn = (dz * cosine + swap_halves(dz * sine)) * gain
    along = jnp.mean(dn * u, axis=-1, keepdims=True) * (inverse * inverse)
    return inverse * (dn - u * along)


def key_message_kernel(*refs):
    sources, (out_ref, *held, sems) = refs[:5], refs[5:]
    me = lax.axis_index("ctx")
    copies = [pltpu.make_async_copy(a, b, sems.at[i]) for i, (a, b) in enumerate(zip(sources, held))]
    for copy in copies:
        copy.start()
    for copy in copies:
        copy.wait()
    k_ref, doc_ref, gain_ref, rows_ref, base_ref = held
    rows, kv_width = k_ref.shape
    hd = gain_ref.shape[1]
    cosine, sine = rotation(rows_ref, base_ref, me)
    marks = jnp.broadcast_to((doc_ref[...] + 1).astype(f32), (meta_rows, rows)).astype(bf16)
    for h in range(kv_width // hd):
        cols = slice(h * hd, (h + 1) * hd)
        u = k_ref[:, cols].astype(f32)
        out_ref[:rows, cols] = norm_rope(u, gain_ref[...], cosine, sine).astype(bf16)
        out_ref[rows:, cols] = marks


def place_marks(dest_ref, blocks):
    rows = dest_ref.shape[1]
    dest = jnp.broadcast_to(dest_ref[...], (meta_rows, rows))
    block = jnp.zeros_like(dest)
    for j in range(1, blocks):
        block = block + (dest >= j * rows).astype(jnp.int32)
    which = lax.broadcasted_iota(jnp.int32, dest.shape, 0)
    return jnp.where(which == 0, block, dest - block * rows).astype(f32).astype(bf16)


def marks_kernel(blocks):
    def body(dest_ref, out_ref):
        out_ref[...] = place_marks(dest_ref, blocks)

    return body


def value_kernel(*refs):
    sources, (out_ref, h_held, w_held, sems) = refs[:2], refs[2:]
    rows, width = h_held.shape
    parts = 8
    part = width // parts
    copies = [pltpu.make_async_copy(sources[0], h_held, sems.at[0])]
    for i in range(parts):
        piece = pl.ds(i * part, part)
        copies.append(
            pltpu.make_async_copy(sources[1].at[piece], w_held.at[piece], sems.at[1 + i])
        )
    for copy in copies:
        copy.start()
    copies[0].wait()
    total = None
    for i in range(parts):
        copies[1 + i].wait()
        piece = slice(i * part, (i + 1) * part)
        product = jnp.dot(h_held[:, piece], w_held[piece], preferred_element_type=f32)
        total = product if total is None else total + product
    out_ref[...] = total.astype(bf16)


def upright_tables(gain_ref, rows_ref, base_ref, scale, held):
    rows = rows_ref.shape[1]
    cosine, sine = rotation(rows_ref, base_ref, lax.axis_index("ctx"))
    held[0] = cosine.T
    held[1] = sine.T
    held[2] = jnp.broadcast_to(gain_ref[...] * scale, (rows, gain_ref.shape[1])).T


def swap_rows(x):
    half = x.shape[0] // 2
    return jnp.concatenate([x[half:], x[:half]], axis=0)


def query_prep_kernel(scale, q_ref, gain_ref, rows_ref, base_ref, scaled_ref, turned_ref, held):
    rows, width = q_ref.shape
    hd = gain_ref.shape[1]

    @pl.when(pl.program_id(0) == 0)
    def _():
        upright_tables(gain_ref, rows_ref, base_ref, scale, held)

    for h in range(width // hd):
        turned = q_ref[:, h * hd : (h + 1) * hd].T
        turned_ref[0, :, h * rows : (h + 1) * rows] = turned
        u = turned.astype(f32)
        inverse = lax.rsqrt(jnp.mean(u * u, axis=0, keepdims=True) + epsilon)
        y = u * inverse * held[2]
        z = y * held[0] + swap_rows(y) * held[1]
        scaled_ref[0, :, h * rows : (h + 1) * rows] = z.astype(bf16)


def share_index(j, half, c, z, core, zs, blocks):
    owner_core = core if half else 1 - core
    return ((z ^ j) * 2 + owner_core) * blocks + c


def arrival_kernel(blocks, zs, dest_hbm, h_hbm, w_hbm, *refs):
    outs, late_outs = refs[:blocks], refs[blocks : 2 * blocks]
    dest_held, h_held, w_held, turned, sems = refs[2 * blocks :]
    me, dp = lax.axis_index("ctx"), lax.axis_index("dp")
    z, core = dp // 2, dp % 2
    parts, rows, part = h_held.shape
    share = turned.shape[0] // (blocks * zs * 2)
    kv_width = w_held.shape[1]
    copies = [pltpu.make_async_copy(dest_hbm, dest_held, sems.at[0])]
    for i in range(parts):
        piece = pl.ds(i * part, part)
        copies.append(pltpu.make_async_copy(h_hbm.at[:, piece], h_held.at[i], sems.at[1 + i]))
    for i in range(parts):
        piece = pl.ds(i * part, part)
        copies.append(
            pltpu.make_async_copy(w_hbm.at[piece], w_held.at[piece], sems.at[1 + parts + i])
        )
    for copy in copies:
        copy.start()
    copies[0].wait()
    marks = place_marks(dest_held, blocks)
    for i in range(parts):
        copies[1 + i].wait()
        for c in range(part // 128):
            at = i * part + c * 128
            turned[at : at + 128] = h_held[i, :, c * 128 : (c + 1) * 128].T
    first = kv_width // 128 * rows + meta_rows
    for m in range(blocks):
        outs[m][first - meta_rows : first] = marks
        c = lax.rem(me + m, blocks)
        for half in range(2):
            for j in range(zs):
                start = share_index(j, half, c, z, core, zs, blocks) * share
                start = pl.multiple_of(start, 16)
                piece = turned[pl.ds(start, share)]
                if half:
                    late_outs[m][j * share : (j + 1) * share] = piece
                else:
                    outs[m][first + j * share : first + (j + 1) * share] = piece
    total = None
    for i in range(parts):
        copies[1 + parts + i].wait()
        product = jnp.dot(
            h_held[i], w_held[i * part : (i + 1) * part], preferred_element_type=f32
        )
        total = product if total is None else total + product
    total = total.astype(bf16)
    for m in range(blocks):
        for h in range(kv_width // 128):
            outs[m][h * rows : (h + 1) * rows] = total[:, h * 128 : (h + 1) * 128]


def mark_rows(ref, rows):
    return ref[rows : rows + meta_rows, :rows].astype(f32)


def arrival_slots(marks, me, blocks, rows):
    marks = marks.astype(f32)
    away = me.astype(f32) - marks[:1]
    away = jnp.where(away < 0, away + blocks, away)
    return away * rows + marks[1:2]


def attend_kernel(back, qs_ref, g_ref, *refs):
    k_refs = refs[: back + 1]
    p_ref, own_ref = refs[back + 1], refs[back + 2]
    send_refs = refs[back + 3 : 2 * back + 3]
    bias_ref = refs[-1]
    rows = g_ref.shape[0]
    hd = own_ref.shape[1]
    group = g_ref.shape[1] // hd

    @pl.when(pl.program_id(0) == 0)
    def _():
        query_doc = mark_rows(k_refs[0], rows)[:1]
        for b in range(back + 1):
            key_doc = jnp.broadcast_to(mark_rows(k_refs[b], rows)[:1], (rows, rows)).T
            allowed = key_doc == query_doc
            if b == 0:
                key_row = lax.broadcasted_iota(jnp.int32, (rows, rows), 0)
                query_row = lax.broadcasted_iota(jnp.int32, (rows, rows), 1)
                allowed = allowed & (key_row <= query_row)
            else:
                allowed = allowed & (lax.axis_index("ctx") >= b)
            bias_ref[b * rows : (b + 1) * rows] = jnp.where(allowed, 0.0, masked)

    keys = jnp.concatenate([r[:rows] for r in k_refs], axis=0)
    logits = jnp.dot(keys, qs_ref[0], preferred_element_type=f32)
    e = jnp.exp2(logits + jnp.concatenate([bias_ref[...]] * group, axis=1))
    p = (e * (1.0 / jnp.sum(e, axis=0, keepdims=True))).astype(bf16)
    p_ref[0] = p
    g = jnp.concatenate([g_ref[:, j * hd : (j + 1) * hd] for j in range(group)], axis=0)
    gv = jnp.dot(p, g, preferred_element_type=f32)
    own_ref[...] = gv[:rows]
    for b in range(back):
        send_refs[b][...] = gv[(b + 1) * rows : (b + 2) * rows].astype(bf16)


def slab_values_kernel(blocks, kv, *refs):
    a_refs, out_ref = refs[:-1], refs[-1]
    me = lax.axis_index("ctx")
    key_count, width = out_ref.shape
    rows = a_refs[0].shape[1]
    first = kv * rows
    slot = lax.broadcasted_iota(jnp.int32, (key_count, rows), 0).astype(f32)
    place, arrived = [], []
    for r in a_refs:
        at = arrival_slots(r[first : first + meta_rows], me, blocks, rows)
        place.append((slot == at).astype(f32).astype(bf16))
        arrived.append(jnp.concatenate([r[h * rows : (h + 1) * rows] for h in range(kv)], axis=1))
    out_ref[...] = jnp.dot(
        jnp.concatenate(place, axis=1), jnp.concatenate(arrived, axis=0), preferred_element_type=f32
    ).astype(bf16)


def backward_kernel(back, factor, p_ref, values_ref, g_ref, u_ref, qs_ref, gain_ref, rows_ref, base_ref, *refs):
    k_refs, refs = refs[: back + 1], refs[back + 1 :]
    gq_ref, own_ref, send_refs, held = refs[0], refs[1], refs[2:-1], refs[-1]
    rows = g_ref.shape[0]
    hd = own_ref.shape[1]
    group = g_ref.shape[1] // hd

    @pl.when(pl.program_id(0) == 0)
    def _():
        upright_tables(gain_ref, rows_ref, base_ref, factor, held)

    g = jnp.concatenate([g_ref[:, j * hd : (j + 1) * hd] for j in range(group)], axis=0)
    dp = lax.dot_general(values_ref[...], g, NT, preferred_element_type=f32)
    p = p_ref[0].astype(f32)
    delta = jnp.sum(p * dp, axis=0, keepdims=True)
    ds = (p * (dp - delta)).astype(bf16)
    gk = lax.dot_general(ds, qs_ref[0], NT, preferred_element_type=f32) * math.log(2.0)
    own_ref[...] = gk[:rows]
    for b in range(back):
        send_refs[b][...] = gk[(b + 1) * rows : (b + 2) * rows].astype(bf16)
    keys = jnp.concatenate([r[:rows] for r in k_refs], axis=0)
    gq = jnp.dot(keys.T, ds, preferred_element_type=f32)
    for j in range(group):
        cols = slice(j * rows, (j + 1) * rows)
        dz, u = gq[:, cols], u_ref[0, :, cols].astype(f32)
        inverse = lax.rsqrt(jnp.mean(u * u, axis=0, keepdims=True) + epsilon)
        dn = (dz * held[0] + swap_rows(dz * held[1])) * held[2]
        along = jnp.mean(dn * u, axis=0, keepdims=True) * (inverse * inverse)
        gq_ref[:, j * hd : (j + 1) * hd] = (inverse * (dn - u * along)).astype(bf16).T


def key_back_kernel(k_ref, own_ref, gain_ref, rows_ref, base_ref, *refs):
    got_refs, out_ref = refs[:-1], refs[-1]
    me = lax.axis_index("ctx")
    hd = gain_ref.shape[1]
    cosine, sine = rotation(rows_ref, base_ref, me)
    total = own_ref[...]
    for r in got_refs:
        total = total + r[...].astype(f32)
    for h in range(k_ref.shape[1] // hd):
        cols = slice(h * hd, (h + 1) * hd)
        u = k_ref[:, cols].astype(f32)
        out_ref[:, cols] = norm_rope_back(u, total[:, cols], gain_ref[...], cosine, sine).astype(bf16)


def gate_kernel(*refs):
    pass


def value_sum_kernel(*refs):
    total = refs[0][...]
    for r in refs[1:-1]:
        total = total + r[...].astype(f32)
    refs[-1][...] = total.astype(bf16)


def pair_kernel(own_ref, got_ref, first_ref, *send_refs):
    share = first_ref.shape[0]
    first_ref[...] = own_ref[:share] + got_ref[:share].astype(f32)
    for j, ref in enumerate(send_refs, 1):
        at = slice(j * share, (j + 1) * share)
        ref[...] = (own_ref[at] + got_ref[at].astype(f32)).astype(bf16)


def total_kernel(first_ref, *refs):
    total = first_ref[...]
    for r in refs[:-1]:
        total = total + r[...].astype(f32)
    refs[-1][...] = total * (1.0 / (lax.axis_size("ctx") * lax.axis_size("dp")))


def hidden_grad_kernel(v_ref, w_ref, out_ref):
    out_ref[...] = lax.dot_general(
        v_ref[...], w_ref[...], NT, preferred_element_type=f32
    ).astype(bf16)


def sibling_weight_kernel(blocks, *refs):
    h_refs, v_refs = refs[:blocks], refs[blocks : 2 * blocks]
    sibling_ref, arrival_ref = refs[2 * blocks :]
    me = lax.axis_index("ctx")
    rows = h_refs[0].shape[1]
    first = h_refs[0].shape[0] - sibling_ref.shape[0]
    slab = jnp.concatenate([r[...] for r in v_refs], axis=0)
    slot = lax.broadcasted_iota(jnp.int32, (blocks * rows, rows), 0).astype(f32)
    for s in range(blocks):
        at = arrival_slots(h_refs[s][first - meta_rows : first], me, blocks, rows)
        place = (slot == at).astype(f32).T.astype(bf16)
        arrived = jnp.dot(place, slab, preferred_element_type=f32).astype(bf16)
        arrival_ref[s * rows : (s + 1) * rows] = arrived
    features = jnp.concatenate([r[first:] for r in h_refs], axis=1)
    sibling_ref[...] = jnp.dot(features, arrival_ref[...], preferred_element_type=f32).astype(bf16)


def own_weight_kernel(*refs):
    h_refs, arrival_ref, own_ref = refs[:-2], refs[-2], refs[-1]
    features = jnp.concatenate([r[...] for r in h_refs], axis=1)
    own_ref[...] = jnp.dot(features, arrival_ref[...], preferred_element_type=f32)


def on_device(hidden, queries, key_states, out_grad, w_value, q_gain, k_gain, dest_rows, doc_ids):
    hidden, queries, key_states, out_grad = hidden[0], queries[0], key_states[0], out_grad[0]
    rows, width = hidden.shape
    hd = q_gain.shape[0]
    kv_width = key_states.shape[1]
    q_width = queries.shape[1]
    kv = kv_width // hd
    group = q_width // kv_width
    blocks, dp_count = lax.axis_size("ctx"), lax.axis_size("dp")
    zs = dp_count // 2
    back = blocks // 2
    factor = hd ** (-0.5)
    share = width // (blocks * dp_count)
    spread = group * rows
    key_count = (back + 1) * rows
    message = jax.ShapeDtypeStruct((rows + meta_rows, kv_width), bf16)
    rows_table, base_table = (jnp.asarray(t) for t in rope_constants(rows, blocks, hd))
    q_gain, k_gain = q_gain[None], k_gain[None]

    def around(array, m):
        return lax.ppermute(array, "ctx", [(i, (i + m) % blocks) for i in range(blocks)])

    def call(kernel, out_shape, name, operands, mib, flops=0, nbytes=0, in_specs=None, after=(), **kw):
        if in_specs is None:
            in_specs = [pl.BlockSpec(memory_space=VMEM)] * len(operands)
        return pl.pallas_call(
            ordered(kernel, len(operands), len(after)), out_shape=out_shape, name=name,
            compiler_params=params(mib), cost_estimate=cost(flops, nbytes),
            in_specs=list(in_specs) + [pl.BlockSpec(memory_space=pl.ANY)] * len(after), **kw,
        )(*operands, *after)

    def in_hbm(array):
        return pltpu.with_memory_space_constraint(array, pltpu.HBM)

    def gate(arrays, after, name):
        return pl.pallas_call(
            gate_kernel, name=name, compiler_params=params(1), cost_estimate=cost(0, 0),
            out_shape=[jax.ShapeDtypeStruct(a.shape, a.dtype) for a in arrays],
            in_specs=[pl.BlockSpec(memory_space=pl.ANY)] * (len(arrays) + len(after)),
            out_specs=[pl.BlockSpec(memory_space=pl.ANY)] * len(arrays),
            input_output_aliases={i: i for i in range(len(arrays))},
        )(*arrays, *after)

    def whole(shape):
        return pl.BlockSpec(shape, lambda h: (0,) * len(shape))

    sources = [in_hbm(a) for a in (key_states, doc_ids, k_gain, rows_table, base_table)]
    key_own = call(
        key_message_kernel, message, "key_message", sources, 4, 0, 1e6,
        in_specs=[pl.BlockSpec(memory_space=pltpu.HBM)] * 5,
        scratch_shapes=[VMEM(a.shape, a.dtype) for a in sources] + [pltpu.SemaphoreType.DMA((5,))],
    )
    key_messages = [key_own] + [around(key_own, m) for m in range(1, back + 1)]

    head_cols = pl.BlockSpec((rows, group * hd), lambda h: (0, h))
    head_set = pl.BlockSpec((1, hd, spread), lambda h: (h, 0, 0))
    message_cols = pl.BlockSpec((rows + meta_rows, hd), lambda h: (0, h))
    row_cols = pl.BlockSpec((rows, hd), lambda h: (0, h))
    table_specs = [whole((1, hd)), whole(rows_table.shape), whole(base_table.shape)]
    upright = VMEM((3, hd, rows), f32)

    half = width // blocks // 2
    length = kv * rows + meta_rows + half
    sources = [in_hbm(a) for a in (dest_rows, hidden, w_value)]
    if share % 16 == 0:
        arrivals = call(
            functools.partial(arrival_kernel, blocks, zs),
            [jax.ShapeDtypeStruct((length, hd), bf16)] * blocks
            + [jax.ShapeDtypeStruct((half, hd), bf16)] * blocks,
            "arrivals", sources, 24, 2 * rows * width * kv_width, 9e6,
            in_specs=[pl.BlockSpec(memory_space=pltpu.HBM)] * 3, after=(key_own,),
            scratch_shapes=[
                VMEM((1, rows), jnp.int32),
                VMEM((8, rows, width // 8), bf16),
                VMEM((width, kv_width), bf16),
                VMEM((width, rows), bf16),
                pltpu.SemaphoreType.DMA((17,)),
            ],
        )
    else:
        me, dp = lax.axis_index("ctx"), lax.axis_index("dp")
        turned = hidden.T.reshape(dp_count * blocks, share, rows)
        value_own = call(
            value_kernel, jax.ShapeDtypeStruct((rows, kv_width), bf16), "value", sources[1:], 16,
            2 * rows * width * kv_width, 7e6,
            in_specs=[pl.BlockSpec(memory_space=pltpu.HBM)] * 2,
            scratch_shapes=[VMEM(a.shape, a.dtype) for a in sources[1:]]
            + [pltpu.SemaphoreType.DMA((9,))],
        )
        marks = call(
            marks_kernel(blocks), jax.ShapeDtypeStruct((meta_rows, rows), bf16), "marks", (dest_rows,), 1
        )
        head_values = [value_own[:, h * hd : (h + 1) * hd] for h in range(kv)]
        arrivals, late = [], []
        for m in range(blocks):
            at = [
                share_index(j, half, lax.rem(me + m, blocks), dp // 2, dp % 2, zs, blocks)
                for half in range(2)
                for j in range(zs)
            ]
            pieces = [lax.dynamic_index_in_dim(turned, place, axis=0) for place in at]
            pieces = jnp.concatenate(pieces, axis=0).reshape(width // blocks, rows)
            arrivals.append(jnp.concatenate([*head_values, marks, pieces[:half]], axis=0))
            late.append(pieces[half:])
        arrivals = arrivals + late
    arrivals, late = arrivals[:blocks], arrivals[blocks:]
    first_arrival = arrivals[0]
    q_scaled, q_turned = call(
        functools.partial(query_prep_kernel, factor * math.log2(math.e)),
        [jax.ShapeDtypeStruct((kv, hd, spread), bf16)] * 2,
        "query_prep", (queries, q_gain, rows_table, base_table), 8, 0, 4e6, grid=(kv,),
        in_specs=[head_cols] + table_specs, out_specs=[head_set] * 2, scratch_shapes=[upright],
        after=(first_arrival,),
    )

    leaving = gate(arrivals[1:], tuple(key_messages[1:]), "arrivals_leave")
    arrivals = [first_arrival] + [around(leaving[m - 1], m) for m in range(1, blocks)]

    attended = call(
        functools.partial(attend_kernel, back),
        [
            jax.ShapeDtypeStruct((kv, key_count, spread), bf16),
            jax.ShapeDtypeStruct((rows, kv_width), f32),
        ]
        + [jax.ShapeDtypeStruct((rows, kv_width), bf16)] * back,
        "attend", (q_scaled, out_grad, *key_messages), 16,
        8 * kv * key_count * spread * hd, 5e6, grid=(kv,),
        in_specs=[head_set, head_cols] + [message_cols] * (back + 1),
        out_specs=[pl.BlockSpec((1, key_count, spread), lambda h: (h, 0, 0))]
        + [row_cols] * (back + 1),
        scratch_shapes=[VMEM((key_count, rows), f32)], after=(leaving[0],),
    )
    probabilities, value_total = attended[0], attended[1]
    value_got = [around(attended[1 + m], blocks - m) for m in range(1, back + 1)]

    slab_values = call(
        functools.partial(slab_values_kernel, blocks, kv),
        jax.ShapeDtypeStruct((key_count, kv_width), bf16), "slab_values", arrivals, 16,
        2 * key_count * blocks * rows * kv_width, 2e6, after=(value_total,),
    )
    value_grad = call(
        value_sum_kernel, jax.ShapeDtypeStruct((rows, kv_width), bf16), "value_sum",
        (value_total, *value_got), 4, 0, 1e6, after=(slab_values,),
    )
    late_leaving = gate(late[1:], (value_grad,), "late_leave")
    late = [late[0]] + [around(late_leaving[m - 1], m) for m in range(1, blocks)]
    value_grads = [value_grad] + [around(value_grad, m) for m in range(1, blocks)]

    backed = call(
        functools.partial(backward_kernel, back, factor),
        [
            jax.ShapeDtypeStruct((rows, q_width), bf16),
            jax.ShapeDtypeStruct((rows, kv_width), f32),
        ]
        + [jax.ShapeDtypeStruct((rows, kv_width), bf16)] * back,
        "backward",
        (
            probabilities, slab_values, out_grad, q_turned, q_scaled, q_gain, rows_table, base_table,
            *key_messages,
        ),
        20, 12 * kv * key_count * spread * hd, 7e6, grid=(kv,),
        in_specs=[
            pl.BlockSpec((1, key_count, spread), lambda h: (h, 0, 0)),
            pl.BlockSpec((key_count, hd), lambda h: (0, h)),
            head_cols, head_set, head_set,
        ]
        + table_specs + [message_cols] * (back + 1),
        out_specs=[head_cols] + [row_cols] * (back + 1),
        scratch_shapes=[upright],
        after=(value_grad,),
    )
    sibling, arrival = call(
        functools.partial(sibling_weight_kernel, blocks),
        [
            jax.ShapeDtypeStruct((half, kv_width), bf16),
            jax.ShapeDtypeStruct((blocks * rows, kv_width), bf16),
        ],
        "sibling_weight", (*arrivals, *value_grads), 16, width * rows * kv_width, 4e6,
        after=(backed[1], *late[1:]),
    )
    own = call(
        own_weight_kernel, jax.ShapeDtypeStruct((half, kv_width), f32), "own_weight",
        (*late, arrival), 16, width * rows * kv_width, 3e6,
    )
    got = lax.ppermute(sibling, "dp", [(d, d ^ 1) for d in range(dp_count)])

    slice_width = width // 4
    hidden_grad = call(
        hidden_grad_kernel, jax.ShapeDtypeStruct((rows, width), bf16),
        "hidden_grad", (value_grad, w_value), 8, 2 * rows * width * kv_width, 7e6,
        grid=(width // slice_width,),
        in_specs=[whole((rows, kv_width)), pl.BlockSpec((slice_width, kv_width), lambda i: (i, 0))],
        out_specs=pl.BlockSpec((rows, slice_width), lambda i: (0, i)),
        after=(),
    )

    pairs = call(
        pair_kernel,
        [jax.ShapeDtypeStruct((share, kv_width), f32)]
        + [jax.ShapeDtypeStruct((share, kv_width), bf16)] * (zs - 1),
        "pair", (own, got), 12, 0, 3e6,
    )
    sums = []
    for j in range(1, zs):
        route = [(z * 2 + c, (z ^ j) * 2 + c) for z in range(zs) for c in range(2)]
        sums.append(lax.ppermute(pairs[j], "dp", route))

    query_grad = backed[0]
    key_leaving = gate(backed[2:], (pairs[0],), "keys_leave")
    key_got = [around(key_leaving[m - 1], blocks - m) for m in range(1, back + 1)]
    weight_grad = call(
        total_kernel, jax.ShapeDtypeStruct((share, kv_width), f32), "total",
        (pairs[0], *sums), 4, 0, 1e6,
    )
    key_grad = call(
        key_back_kernel, jax.ShapeDtypeStruct((rows, kv_width), bf16), "key_back",
        (key_states, backed[1], k_gain, rows_table, base_table, *key_got), 4, 0, 1e6,
    )
    return (hidden_grad[None], query_grad[None], key_grad[None], weight_grad)


def solution(mesh):
    return jax.shard_map(
        on_device,
        mesh=mesh,
        in_specs=(
            P("dp", "ctx", None),
            P("dp", "ctx", None),
            P("dp", "ctx", None),
            P("dp", "ctx", None),
            P(),
            P(),
            P(),
            P("dp", "ctx"),
            P("dp", "ctx"),
        ),
        out_specs=(
            P("dp", "ctx", None),
            P("dp", "ctx", None),
            P("dp", "ctx", None),
            P(("dp", "ctx"), None),
        ),
        check_vma=False,
    )
```

```python
import functools
import math

import jax
import jax.numpy as jnp
import numpy as np
from jax import lax
from jax.experimental import pallas as pl
from jax.experimental.pallas import tpu as pltpu
from jax.sharding import PartitionSpec as P

epsilon = 1e-06
rope_base = 1000000.0
meta_rows = 16
masked = -1e30
VMEM = pltpu.VMEM
f32, bf16 = jnp.float32, jnp.bfloat16
NT = (((1,), (1,)), ((), ()))


def params(mib):
    return pltpu.CompilerParams(vmem_limit_bytes=mib << 20)


def ordered(kernel, inputs, after):
    def body(*refs):
        kernel(*refs[:inputs], *refs[inputs + after :])

    return body


def cost(flops, bytes_accessed):
    return pl.CostEstimate(flops=int(flops), bytes_accessed=int(bytes_accessed), transcendentals=0)


def rope_constants(rows, blocks, head_width):
    half = head_width // 2
    frequency = rope_base ** (-(np.arange(half) * 2.0 / head_width))
    frequency = np.concatenate([frequency, frequency])
    sign = np.concatenate([-np.ones(half), np.ones(half)])

    def table(positions):
        angles = positions[:, None] * frequency[None, :]
        return np.stack([np.cos(angles), np.sin(angles) * sign]).astype(np.float32)

    return table(np.arange(rows)), table(np.arange(blocks) * rows)


def rotation(rows_ref, base_ref, me):
    cos_b = base_ref[0, pl.ds(me, 1), :]
    sin_b = base_ref[1, pl.ds(me, 1), :]
    cos_r, sin_r = rows_ref[0], rows_ref[1]
    return cos_b * cos_r - sin_b * sin_r, sin_b * cos_r + cos_b * sin_r


def swap_halves(x):
    return pltpu.roll(x, x.shape[-1] // 2, 1)


def norm_rope(u, gain, cosine, sine):
    inverse = lax.rsqrt(jnp.mean(u * u, axis=-1, keepdims=True) + epsilon)
    y = u * inverse * gain
    return y * cosine + swap_halves(y) * sine


def norm_rope_back(u, dz, gain, cosine, sine):
    inverse = lax.rsqrt(jnp.mean(u * u, axis=-1, keepdims=True) + epsilon)
    dn = (dz * cosine + swap_halves(dz * sine)) * gain
    along = jnp.mean(dn * u, axis=-1, keepdims=True) * (inverse * inverse)
    return inverse * (dn - u * along)


def key_message_kernel(*refs):
    sources, (out_ref, *held, sems) = refs[:5], refs[5:]
    me = lax.axis_index("ctx")
    copies = [pltpu.make_async_copy(a, b, sems.at[i]) for i, (a, b) in enumerate(zip(sources, held))]
    for copy in copies:
        copy.start()
    for copy in copies:
        copy.wait()
    k_ref, doc_ref, gain_ref, rows_ref, base_ref = held
    rows, kv_width = k_ref.shape
    hd = gain_ref.shape[1]
    cosine, sine = rotation(rows_ref, base_ref, me)
    marks = jnp.broadcast_to((doc_ref[...] + 1).astype(f32), (meta_rows, rows)).astype(bf16)
    for h in range(kv_width // hd):
        cols = slice(h * hd, (h + 1) * hd)
        u = k_ref[:, cols].astype(f32)
        out_ref[:rows, cols] = norm_rope(u, gain_ref[...], cosine, sine).astype(bf16)
        out_ref[rows:, cols] = marks


def place_marks(dest_ref, blocks):
    rows = dest_ref.shape[1]
    dest = jnp.broadcast_to(dest_ref[...], (meta_rows, rows))
    block = jnp.zeros_like(dest)
    for j in range(1, blocks):
        block = block + (dest >= j * rows).astype(jnp.int32)
    which = lax.broadcasted_iota(jnp.int32, dest.shape, 0)
    return jnp.where(which == 0, block, dest - block * rows).astype(f32).astype(bf16)


def marks_kernel(blocks):
    def body(dest_ref, out_ref):
        out_ref[...] = place_marks(dest_ref, blocks)

    return body


def value_kernel(*refs):
    sources, (out_ref, h_held, w_held, sems) = refs[:2], refs[2:]
    rows, width = h_held.shape
    parts = 8
    part = width // parts
    copies = [pltpu.make_async_copy(sources[0], h_held, sems.at[0])]
    for i in range(parts):
        piece = pl.ds(i * part, part)
        copies.append(
            pltpu.make_async_copy(sources[1].at[piece], w_held.at[piece], sems.at[1 + i])
        )
    for copy in copies:
        copy.start()
    copies[0].wait()
    total = None
    for i in range(parts):
        copies[1 + i].wait()
        piece = slice(i * part, (i + 1) * part)
        product = jnp.dot(h_held[:, piece], w_held[piece], preferred_element_type=f32)
        total = product if total is None else total + product
    out_ref[...] = total.astype(bf16)


def upright_tables(gain_ref, rows_ref, base_ref, scale, held):
    rows = rows_ref.shape[1]
    cosine, sine = rotation(rows_ref, base_ref, lax.axis_index("ctx"))
    held[0] = cosine.T
    held[1] = sine.T
    held[2] = jnp.broadcast_to(gain_ref[...] * scale, (rows, gain_ref.shape[1])).T


def swap_rows(x):
    half = x.shape[0] // 2
    return jnp.concatenate([x[half:], x[:half]], axis=0)


def query_prep_kernel(scale, q_ref, gain_ref, rows_ref, base_ref, scaled_ref, turned_ref, held):
    rows, width = q_ref.shape
    hd = gain_ref.shape[1]

    @pl.when(pl.program_id(0) == 0)
    def _():
        upright_tables(gain_ref, rows_ref, base_ref, scale, held)

    for h in range(width // hd):
        turned = q_ref[:, h * hd : (h + 1) * hd].T
        turned_ref[0, :, h * rows : (h + 1) * rows] = turned
        u = turned.astype(f32)
        inverse = lax.rsqrt(jnp.mean(u * u, axis=0, keepdims=True) + epsilon)
        y = u * inverse * held[2]
        z = y * held[0] + swap_rows(y) * held[1]
        scaled_ref[0, :, h * rows : (h + 1) * rows] = z.astype(bf16)


def share_index(j, half, c, z, core, zs, blocks):
    owner_core = core if half else 1 - core
    return ((z ^ j) * 2 + owner_core) * blocks + c


def arrival_kernel(blocks, zs, dest_hbm, h_hbm, w_hbm, *refs):
    outs, late_outs = refs[:blocks], refs[blocks : 2 * blocks]
    dest_held, h_held, w_held, turned, sems = refs[2 * blocks :]
    me, dp = lax.axis_index("ctx"), lax.axis_index("dp")
    z, core = dp // 2, dp % 2
    parts, rows, part = h_held.shape
    share = turned.shape[0] // (blocks * zs * 2)
    kv_width = w_held.shape[1]
    copies = [pltpu.make_async_copy(dest_hbm, dest_held, sems.at[0])]
    for i in range(parts):
        piece = pl.ds(i * part, part)
        copies.append(pltpu.make_async_copy(h_hbm.at[:, piece], h_held.at[i], sems.at[1 + i]))
    for i in range(parts):
        piece = pl.ds(i * part, part)
        copies.append(
            pltpu.make_async_copy(w_hbm.at[piece], w_held.at[piece], sems.at[1 + parts + i])
        )
    for copy in copies:
        copy.start()
    copies[0].wait()
    marks = place_marks(dest_held, blocks)
    for i in range(parts):
        copies[1 + i].wait()
        for c in range(part // 128):
            at = i * part + c * 128
            turned[at : at + 128] = h_held[i, :, c * 128 : (c + 1) * 128].T
    first = kv_width // 128 * rows + meta_rows
    for m in range(blocks):
        outs[m][first - meta_rows : first] = marks
        c = lax.rem(me + m, blocks)
        for half in range(2):
            for j in range(zs):
                start = share_index(j, half, c, z, core, zs, blocks) * share
                start = pl.multiple_of(start, 16)
                piece = turned[pl.ds(start, share)]
                if half:
                    late_outs[m][j * share : (j + 1) * share] = piece
                else:
                    outs[m][first + j * share : first + (j + 1) * share] = piece
    total = None
    for i in range(parts):
        copies[1 + parts + i].wait()
        product = jnp.dot(
            h_held[i], w_held[i * part : (i + 1) * part], preferred_element_type=f32
        )
        total = product if total is None else total + product
    total = total.astype(bf16)
    for m in range(blocks):
        for h in range(kv_width // 128):
            outs[m][h * rows : (h + 1) * rows] = total[:, h * 128 : (h + 1) * 128]


def mark_rows(ref, rows):
    return ref[rows : rows + meta_rows, :rows].astype(f32)


def arrival_slots(marks, me, blocks, rows):
    marks = marks.astype(f32)
    away = me.astype(f32) - marks[:1]
    away = jnp.where(away < 0, away + blocks, away)
    return away * rows + marks[1:2]


def attend_kernel(back, qs_ref, g_ref, *refs):
    k_refs = refs[: back + 1]
    p_ref, own_ref = refs[back + 1], refs[back + 2]
    send_refs = refs[back + 3 : 2 * back + 3]
    bias_ref = refs[-1]
    rows = g_ref.shape[0]
    hd = own_ref.shape[1]
    group = g_ref.shape[1] // hd

    @pl.when(pl.program_id(0) == 0)
    def _():
        query_doc = mark_rows(k_refs[0], rows)[:1]
        for b in range(back + 1):
            key_doc = jnp.broadcast_to(mark_rows(k_refs[b], rows)[:1], (rows, rows)).T
            allowed = key_doc == query_doc
            if b == 0:
                key_row = lax.broadcasted_iota(jnp.int32, (rows, rows), 0)
                query_row = lax.broadcasted_iota(jnp.int32, (rows, rows), 1)
                allowed = allowed & (key_row <= query_row)
            else:
                allowed = allowed & (lax.axis_index("ctx") >= b)
            bias_ref[b * rows : (b + 1) * rows] = jnp.where(allowed, 0.0, masked)

    keys = jnp.concatenate([r[:rows] for r in k_refs], axis=0)
    logits = jnp.dot(keys, qs_ref[0], preferred_element_type=f32)
    e = jnp.exp2(logits + jnp.concatenate([bias_ref[...]] * group, axis=1))
    p = (e * (1.0 / jnp.sum(e, axis=0, keepdims=True))).astype(bf16)
    p_ref[0] = p
    g = jnp.concatenate([g_ref[:, j * hd : (j + 1) * hd] for j in range(group)], axis=0)
    gv = jnp.dot(p, g, preferred_element_type=f32)
    own_ref[...] = gv[:rows]
    for b in range(back):
        send_refs[b][...] = gv[(b + 1) * rows : (b + 2) * rows].astype(bf16)


def slab_values_kernel(blocks, kv, *refs):
    a_refs, out_ref = refs[:-1], refs[-1]
    me = lax.axis_index("ctx")
    key_count, width = out_ref.shape
    rows = a_refs[0].shape[1]
    first = kv * rows
    slot = lax.broadcasted_iota(jnp.int32, (key_count, rows), 0).astype(f32)
    place, arrived = [], []
    for r in a_refs:
        at = arrival_slots(r[first : first + meta_rows], me, blocks, rows)
        place.append((slot == at).astype(f32).astype(bf16))
        arrived.append(jnp.concatenate([r[h * rows : (h + 1) * rows] for h in range(kv)], axis=1))
    out_ref[...] = jnp.dot(
        jnp.concatenate(place, axis=1), jnp.concatenate(arrived, axis=0), preferred_element_type=f32
    ).astype(bf16)


def backward_kernel(back, factor, p_ref, values_ref, g_ref, u_ref, qs_ref, gain_ref, rows_ref, base_ref, *refs):
    k_refs, refs = refs[: back + 1], refs[back + 1 :]
    gq_ref, own_ref, send_refs, held = refs[0], refs[1], refs[2:-1], refs[-1]
    rows = g_ref.shape[0]
    hd = own_ref.shape[1]
    group = g_ref.shape[1] // hd

    @pl.when(pl.program_id(0) == 0)
    def _():
        upright_tables(gain_ref, rows_ref, base_ref, factor, held)

    g = jnp.concatenate([g_ref[:, j * hd : (j + 1) * hd] for j in range(group)], axis=0)
    dp = lax.dot_general(values_ref[...], g, NT, preferred_element_type=f32)
    p = p_ref[0].astype(f32)
    delta = jnp.sum(p * dp, axis=0, keepdims=True)
    ds = (p * (dp - delta)).astype(bf16)
    gk = lax.dot_general(ds, qs_ref[0], NT, preferred_element_type=f32) * math.log(2.0)
    own_ref[...] = gk[:rows]
    for b in range(back):
        send_refs[b][...] = gk[(b + 1) * rows : (b + 2) * rows].astype(bf16)
    keys = jnp.concatenate([r[:rows] for r in k_refs], axis=0)
    gq = jnp.dot(keys.T, ds, preferred_element_type=f32)
    for j in range(group):
        cols = slice(j * rows, (j + 1) * rows)
        dz, u = gq[:, cols], u_ref[0, :, cols].astype(f32)
        inverse = lax.rsqrt(jnp.mean(u * u, axis=0, keepdims=True) + epsilon)
        dn = (dz * held[0] + swap_rows(dz * held[1])) * held[2]
        along = jnp.mean(dn * u, axis=0, keepdims=True) * (inverse * inverse)
        gq_ref[:, j * hd : (j + 1) * hd] = (inverse * (dn - u * along)).astype(bf16).T


def key_back_kernel(k_ref, own_ref, gain_ref, rows_ref, base_ref, *refs):
    got_refs, out_ref = refs[:-1], refs[-1]
    me = lax.axis_index("ctx")
    hd = gain_ref.shape[1]
    cosine, sine = rotation(rows_ref, base_ref, me)
    total = own_ref[...]
    for r in got_refs:
        total = total + r[...].astype(f32)
    for h in range(k_ref.shape[1] // hd):
        cols = slice(h * hd, (h + 1) * hd)
        u = k_ref[:, cols].astype(f32)
        out_ref[:, cols] = norm_rope_back(u, total[:, cols], gain_ref[...], cosine, sine).astype(bf16)


def gate_kernel(*refs):
    pass


def value_sum_kernel(back, total_ref, *refs):
    got_refs, refs = refs[:back], refs[back:]
    count = len(refs) // 2
    late_refs, grad_ref, send_refs = refs[:count], refs[count], refs[count + 1 :]
    total = total_ref[...]
    for r in got_refs:
        total = total + r[...].astype(f32)
    grad = total.astype(bf16)
    grad_ref[...] = grad
    rows, width = grad.shape
    for late_ref, send_ref in zip(late_refs, send_refs):
        for h in range(width // 128):
            send_ref[h * rows : (h + 1) * rows] = grad[:, h * 128 : (h + 1) * 128]
        send_ref[width // 128 * rows :] = late_ref[...]


def pair_kernel(own_ref, got_ref, first_ref, *send_refs):
    share = first_ref.shape[0]
    first_ref[...] = own_ref[:share] + got_ref[:share].astype(f32)
    for j, ref in enumerate(send_refs, 1):
        at = slice(j * share, (j + 1) * share)
        ref[...] = (own_ref[at] + got_ref[at].astype(f32)).astype(bf16)


def total_kernel(first_ref, *refs):
    total = first_ref[...]
    for r in refs[:-1]:
        total = total + r[...].astype(f32)
    refs[-1][...] = total * (1.0 / (lax.axis_size("ctx") * lax.axis_size("dp")))


def hidden_grad_kernel(v_ref, w_ref, out_ref):
    out_ref[...] = lax.dot_general(
        v_ref[...], w_ref[...], NT, preferred_element_type=f32
    ).astype(bf16)


def sibling_weight_kernel(blocks, *refs):
    h_refs, v_refs = refs[:blocks], refs[blocks : 2 * blocks]
    sibling_ref, arrival_ref = refs[2 * blocks :]
    heads = v_refs[0].shape[1] // 128
    me = lax.axis_index("ctx")
    rows = h_refs[0].shape[1]
    first = h_refs[0].shape[0] - sibling_ref.shape[0]
    slab = [v_refs[0][...]]
    for r in v_refs[1:]:
        slab.append(jnp.concatenate([r[h * rows : (h + 1) * rows] for h in range(heads)], axis=1))
    slab = jnp.concatenate(slab, axis=0)
    slot = lax.broadcasted_iota(jnp.int32, (blocks * rows, rows), 0).astype(f32)
    for s in range(blocks):
        at = arrival_slots(h_refs[s][first - meta_rows : first], me, blocks, rows)
        place = (slot == at).astype(f32).T.astype(bf16)
        arrived = jnp.dot(place, slab, preferred_element_type=f32).astype(bf16)
        arrival_ref[s * rows : (s + 1) * rows] = arrived
    features = jnp.concatenate([r[first:] for r in h_refs], axis=1)
    sibling_ref[...] = jnp.dot(features, arrival_ref[...], preferred_element_type=f32).astype(bf16)


def own_weight_kernel(*refs):
    h_refs, arrival_ref, own_ref = refs[:-2], refs[-2], refs[-1]
    half = own_ref.shape[0]
    features = jnp.concatenate([r[r.shape[0] - half :] for r in h_refs], axis=1)
    own_ref[...] = jnp.dot(features, arrival_ref[...], preferred_element_type=f32)


def on_device(hidden, queries, key_states, out_grad, w_value, q_gain, k_gain, dest_rows, doc_ids):
    hidden, queries, key_states, out_grad = hidden[0], queries[0], key_states[0], out_grad[0]
    rows, width = hidden.shape
    hd = q_gain.shape[0]
    kv_width = key_states.shape[1]
    q_width = queries.shape[1]
    kv = kv_width // hd
    group = q_width // kv_width
    blocks, dp_count = lax.axis_size("ctx"), lax.axis_size("dp")
    zs = dp_count // 2
    back = blocks // 2
    factor = hd ** (-0.5)
    share = width // (blocks * dp_count)
    spread = group * rows
    key_count = (back + 1) * rows
    message = jax.ShapeDtypeStruct((rows + meta_rows, kv_width), bf16)
    rows_table, base_table = (jnp.asarray(t) for t in rope_constants(rows, blocks, hd))
    q_gain, k_gain = q_gain[None], k_gain[None]

    def around(array, m):
        return lax.ppermute(array, "ctx", [(i, (i + m) % blocks) for i in range(blocks)])

    def call(kernel, out_shape, name, operands, mib, flops=0, nbytes=0, in_specs=None, after=(), **kw):
        if in_specs is None:
            in_specs = [pl.BlockSpec(memory_space=VMEM)] * len(operands)
        return pl.pallas_call(
            ordered(kernel, len(operands), len(after)), out_shape=out_shape, name=name,
            compiler_params=params(mib), cost_estimate=cost(flops, nbytes),
            in_specs=list(in_specs) + [pl.BlockSpec(memory_space=pl.ANY)] * len(after), **kw,
        )(*operands, *after)

    def in_hbm(array):
        return pltpu.with_memory_space_constraint(array, pltpu.HBM)

    def gate(arrays, after, name):
        return pl.pallas_call(
            gate_kernel, name=name, compiler_params=params(1), cost_estimate=cost(0, 0),
            out_shape=[jax.ShapeDtypeStruct(a.shape, a.dtype) for a in arrays],
            in_specs=[pl.BlockSpec(memory_space=pl.ANY)] * (len(arrays) + len(after)),
            out_specs=[pl.BlockSpec(memory_space=pl.ANY)] * len(arrays),
            input_output_aliases={i: i for i in range(len(arrays))},
        )(*arrays, *after)

    def whole(shape):
        return pl.BlockSpec(shape, lambda h: (0,) * len(shape))

    sources = [in_hbm(a) for a in (key_states, doc_ids, k_gain, rows_table, base_table)]
    key_own = call(
        key_message_kernel, message, "key_message", sources, 4, 0, 1e6,
        in_specs=[pl.BlockSpec(memory_space=pltpu.HBM)] * 5,
        scratch_shapes=[VMEM(a.shape, a.dtype) for a in sources] + [pltpu.SemaphoreType.DMA((5,))],
    )
    key_messages = [key_own] + [around(key_own, m) for m in range(1, back + 1)]

    head_cols = pl.BlockSpec((rows, group * hd), lambda h: (0, h))
    head_set = pl.BlockSpec((1, hd, spread), lambda h: (h, 0, 0))
    message_cols = pl.BlockSpec((rows + meta_rows, hd), lambda h: (0, h))
    row_cols = pl.BlockSpec((rows, hd), lambda h: (0, h))
    table_specs = [whole((1, hd)), whole(rows_table.shape), whole(base_table.shape)]
    upright = VMEM((3, hd, rows), f32)

    half = width // blocks // 2
    length = kv * rows + meta_rows + half
    sources = [in_hbm(a) for a in (dest_rows, hidden, w_value)]
    if share % 16 == 0:
        arrivals = call(
            functools.partial(arrival_kernel, blocks, zs),
            [jax.ShapeDtypeStruct((length, hd), bf16)] * blocks
            + [jax.ShapeDtypeStruct((half, hd), bf16)] * blocks,
            "arrivals", sources, 24, 2 * rows * width * kv_width, 9e6,
            in_specs=[pl.BlockSpec(memory_space=pltpu.HBM)] * 3, after=(key_own,),
            scratch_shapes=[
                VMEM((1, rows), jnp.int32),
                VMEM((8, rows, width // 8), bf16),
                VMEM((width, kv_width), bf16),
                VMEM((width, rows), bf16),
                pltpu.SemaphoreType.DMA((17,)),
            ],
        )
    else:
        me, dp = lax.axis_index("ctx"), lax.axis_index("dp")
        turned = hidden.T.reshape(dp_count * blocks, share, rows)
        value_own = call(
            value_kernel, jax.ShapeDtypeStruct((rows, kv_width), bf16), "value", sources[1:], 16,
            2 * rows * width * kv_width, 7e6,
            in_specs=[pl.BlockSpec(memory_space=pltpu.HBM)] * 2,
            scratch_shapes=[VMEM(a.shape, a.dtype) for a in sources[1:]]
            + [pltpu.SemaphoreType.DMA((9,))],
        )
        marks = call(
            marks_kernel(blocks), jax.ShapeDtypeStruct((meta_rows, rows), bf16), "marks", (dest_rows,), 1
        )
        head_values = [value_own[:, h * hd : (h + 1) * hd] for h in range(kv)]
        arrivals, late = [], []
        for m in range(blocks):
            at = [
                share_index(j, half, lax.rem(me + m, blocks), dp // 2, dp % 2, zs, blocks)
                for half in range(2)
                for j in range(zs)
            ]
            pieces = [lax.dynamic_index_in_dim(turned, place, axis=0) for place in at]
            pieces = jnp.concatenate(pieces, axis=0).reshape(width // blocks, rows)
            arrivals.append(jnp.concatenate([*head_values, marks, pieces[:half]], axis=0))
            late.append(pieces[half:])
        arrivals = arrivals + late
    arrivals, late = arrivals[:blocks], arrivals[blocks:]
    first_arrival = arrivals[0]
    q_scaled, q_turned = call(
        functools.partial(query_prep_kernel, factor * math.log2(math.e)),
        [jax.ShapeDtypeStruct((kv, hd, spread), bf16)] * 2,
        "query_prep", (queries, q_gain, rows_table, base_table), 8, 0, 4e6, grid=(kv,),
        in_specs=[head_cols] + table_specs, out_specs=[head_set] * 2, scratch_shapes=[upright],
        after=(first_arrival,),
    )

    leaving = gate(arrivals[1:], tuple(key_messages[1:]), "arrivals_leave")
    arrivals = [first_arrival] + [around(leaving[m - 1], m) for m in range(1, blocks)]

    attended = call(
        functools.partial(attend_kernel, back),
        [
            jax.ShapeDtypeStruct((kv, key_count, spread), bf16),
            jax.ShapeDtypeStruct((rows, kv_width), f32),
        ]
        + [jax.ShapeDtypeStruct((rows, kv_width), bf16)] * back,
        "attend", (q_scaled, out_grad, *key_messages), 16,
        8 * kv * key_count * spread * hd, 5e6, grid=(kv,),
        in_specs=[head_set, head_cols] + [message_cols] * (back + 1),
        out_specs=[pl.BlockSpec((1, key_count, spread), lambda h: (h, 0, 0))]
        + [row_cols] * (back + 1),
        scratch_shapes=[VMEM((key_count, rows), f32)], after=(leaving[0],),
    )
    probabilities, value_total = attended[0], attended[1]
    value_got = [around(attended[1 + m], blocks - m) for m in range(1, back + 1)]

    slab_values = call(
        functools.partial(slab_values_kernel, blocks, kv),
        jax.ShapeDtypeStruct((key_count, kv_width), bf16), "slab_values", arrivals, 16,
        2 * key_count * blocks * rows * kv_width, 2e6, after=(value_total,),
    )
    value_grad, *followed = call(
        functools.partial(value_sum_kernel, back),
        [jax.ShapeDtypeStruct((rows, kv_width), bf16)]
        + [jax.ShapeDtypeStruct((kv * rows + half, hd), bf16)] * (blocks - 1),
        "value_sum", (value_total, *value_got, *late[1:]), 8, 0, 3e6, after=(slab_values,),
    )
    followed = [around(followed[m - 1], m) for m in range(1, blocks)]

    backed = call(
        functools.partial(backward_kernel, back, factor),
        [
            jax.ShapeDtypeStruct((rows, q_width), bf16),
            jax.ShapeDtypeStruct((rows, kv_width), f32),
        ]
        + [jax.ShapeDtypeStruct((rows, kv_width), bf16)] * back,
        "backward",
        (
            probabilities, slab_values, out_grad, q_turned, q_scaled, q_gain, rows_table, base_table,
            *key_messages,
        ),
        20, 12 * kv * key_count * spread * hd, 7e6, grid=(kv,),
        in_specs=[
            pl.BlockSpec((1, key_count, spread), lambda h: (h, 0, 0)),
            pl.BlockSpec((key_count, hd), lambda h: (0, h)),
            head_cols, head_set, head_set,
        ]
        + table_specs + [message_cols] * (back + 1),
        out_specs=[head_cols] + [row_cols] * (back + 1),
        scratch_shapes=[upright],
        after=(value_grad,),
    )
    sibling, arrival = call(
        functools.partial(sibling_weight_kernel, blocks),
        [
            jax.ShapeDtypeStruct((half, kv_width), bf16),
            jax.ShapeDtypeStruct((blocks * rows, kv_width), bf16),
        ],
        "sibling_weight", (*arrivals, value_grad, *followed), 16, width * rows * kv_width, 4e6,
        after=(backed[1],),
    )
    own = call(
        own_weight_kernel, jax.ShapeDtypeStruct((half, kv_width), f32), "own_weight",
        (late[0], *followed, arrival), 16, width * rows * kv_width, 3e6,
    )
    got = lax.ppermute(sibling, "dp", [(d, d ^ 1) for d in range(dp_count)])

    slice_width = width // 4
    hidden_grad = call(
        hidden_grad_kernel, jax.ShapeDtypeStruct((rows, width), bf16),
        "hidden_grad", (value_grad, w_value), 8, 2 * rows * width * kv_width, 7e6,
        grid=(width // slice_width,),
        in_specs=[whole((rows, kv_width)), pl.BlockSpec((slice_width, kv_width), lambda i: (i, 0))],
        out_specs=pl.BlockSpec((rows, slice_width), lambda i: (0, i)),
        after=(),
    )

    pairs = call(
        pair_kernel,
        [jax.ShapeDtypeStruct((share, kv_width), f32)]
        + [jax.ShapeDtypeStruct((share, kv_width), bf16)] * (zs - 1),
        "pair", (own, got), 12, 0, 3e6,
    )
    sums = []
    for j in range(1, zs):
        route = [(z * 2 + c, (z ^ j) * 2 + c) for z in range(zs) for c in range(2)]
        sums.append(lax.ppermute(pairs[j], "dp", route))

    query_grad = backed[0]
    key_leaving = gate(backed[2:], (pairs[0],), "keys_leave")
    key_got = [around(key_leaving[m - 1], blocks - m) for m in range(1, back + 1)]
    weight_grad = call(
        total_kernel, jax.ShapeDtypeStruct((share, kv_width), f32), "total",
        (pairs[0], *sums), 4, 0, 1e6,
    )
    key_grad = call(
        key_back_kernel, jax.ShapeDtypeStruct((rows, kv_width), bf16), "key_back",
        (key_states, backed[1], k_gain, rows_table, base_table, *key_got), 4, 0, 1e6,
    )
    return (hidden_grad[None], query_grad[None], key_grad[None], weight_grad)


def solution(mesh):
    return jax.shard_map(
        on_device,
        mesh=mesh,
        in_specs=(
            P("dp", "ctx", None),
            P("dp", "ctx", None),
            P("dp", "ctx", None),
            P("dp", "ctx", None),
            P(),
            P(),
            P(),
            P("dp", "ctx"),
            P("dp", "ctx"),
        ),
        out_specs=(
            P("dp", "ctx", None),
            P("dp", "ctx", None),
            P("dp", "ctx", None),
            P(("dp", "ctx"), None),
        ),
        check_vma=False,
    )
```

```python
import functools
import math

import jax
import jax.numpy as jnp
import numpy as np
from jax import lax
from jax.experimental import pallas as pl
from jax.experimental.pallas import tpu as pltpu
from jax.sharding import PartitionSpec as P

epsilon = 1e-06
rope_base = 1000000.0
meta_rows = 16
masked = -1e30
VMEM = pltpu.VMEM
f32, bf16 = jnp.float32, jnp.bfloat16
NT = (((1,), (1,)), ((), ()))


def params(mib):
    return pltpu.CompilerParams(vmem_limit_bytes=mib << 20)


def ordered(kernel, inputs, after):
    def body(*refs):
        kernel(*refs[:inputs], *refs[inputs + after :])

    return body


def cost(flops, bytes_accessed):
    return pl.CostEstimate(flops=int(flops), bytes_accessed=int(bytes_accessed), transcendentals=0)


def rope_constants(rows, blocks, head_width):
    half = head_width // 2
    frequency = rope_base ** (-(np.arange(half) * 2.0 / head_width))
    frequency = np.concatenate([frequency, frequency])
    sign = np.concatenate([-np.ones(half), np.ones(half)])

    def table(positions):
        angles = positions[:, None] * frequency[None, :]
        return np.stack([np.cos(angles), np.sin(angles) * sign]).astype(np.float32)

    return table(np.arange(rows)), table(np.arange(blocks) * rows)


def rotation(rows_ref, base_ref, me):
    cos_b = base_ref[0, pl.ds(me, 1), :]
    sin_b = base_ref[1, pl.ds(me, 1), :]
    cos_r, sin_r = rows_ref[0], rows_ref[1]
    return cos_b * cos_r - sin_b * sin_r, sin_b * cos_r + cos_b * sin_r


def swap_halves(x):
    return pltpu.roll(x, x.shape[-1] // 2, 1)


def norm_rope(u, gain, cosine, sine):
    inverse = lax.rsqrt(jnp.mean(u * u, axis=-1, keepdims=True) + epsilon)
    y = u * inverse * gain
    return y * cosine + swap_halves(y) * sine


def norm_rope_back(u, dz, gain, cosine, sine):
    inverse = lax.rsqrt(jnp.mean(u * u, axis=-1, keepdims=True) + epsilon)
    dn = (dz * cosine + swap_halves(dz * sine)) * gain
    along = jnp.mean(dn * u, axis=-1, keepdims=True) * (inverse * inverse)
    return inverse * (dn - u * along)


def key_message_kernel(*refs):
    sources, (out_ref, *held, sems) = refs[:5], refs[5:]
    me = lax.axis_index("ctx")
    copies = [pltpu.make_async_copy(a, b, sems.at[i]) for i, (a, b) in enumerate(zip(sources, held))]
    for copy in copies:
        copy.start()
    for copy in copies:
        copy.wait()
    k_ref, doc_ref, gain_ref, rows_ref, base_ref = held
    rows, kv_width = k_ref.shape
    hd = gain_ref.shape[1]
    cosine, sine = rotation(rows_ref, base_ref, me)
    marks = jnp.broadcast_to((doc_ref[...] + 1).astype(f32), (meta_rows, rows)).astype(bf16)
    for h in range(kv_width // hd):
        cols = slice(h * hd, (h + 1) * hd)
        u = k_ref[:, cols].astype(f32)
        out_ref[:rows, cols] = norm_rope(u, gain_ref[...], cosine, sine).astype(bf16)
        out_ref[rows:, cols] = marks


def place_marks(dest_ref, blocks):
    rows = dest_ref.shape[1]
    dest = jnp.broadcast_to(dest_ref[...], (meta_rows, rows))
    block = jnp.zeros_like(dest)
    for j in range(1, blocks):
        block = block + (dest >= j * rows).astype(jnp.int32)
    which = lax.broadcasted_iota(jnp.int32, dest.shape, 0)
    return jnp.where(which == 0, block, dest - block * rows).astype(f32).astype(bf16)


def marks_kernel(blocks):
    def body(dest_ref, out_ref):
        out_ref[...] = place_marks(dest_ref, blocks)

    return body


def value_kernel(*refs):
    sources, (out_ref, h_held, w_held, sems) = refs[:2], refs[2:]
    rows, width = h_held.shape
    parts = 8
    part = width // parts
    copies = [pltpu.make_async_copy(sources[0], h_held, sems.at[0])]
    for i in range(parts):
        piece = pl.ds(i * part, part)
        copies.append(
            pltpu.make_async_copy(sources[1].at[piece], w_held.at[piece], sems.at[1 + i])
        )
    for copy in copies:
        copy.start()
    copies[0].wait()
    total = None
    for i in range(parts):
        copies[1 + i].wait()
        piece = slice(i * part, (i + 1) * part)
        product = jnp.dot(h_held[:, piece], w_held[piece], preferred_element_type=f32)
        total = product if total is None else total + product
    out_ref[...] = total.astype(bf16)


def upright_tables(gain_ref, rows_ref, base_ref, scale, held):
    rows = rows_ref.shape[1]
    cosine, sine = rotation(rows_ref, base_ref, lax.axis_index("ctx"))
    held[0] = cosine.T
    held[1] = sine.T
    held[2] = jnp.broadcast_to(gain_ref[...] * scale, (rows, gain_ref.shape[1])).T


def swap_rows(x):
    half = x.shape[0] // 2
    return jnp.concatenate([x[half:], x[:half]], axis=0)


def query_prep_kernel(scale, q_ref, gain_ref, rows_ref, base_ref, scaled_ref, turned_ref, held):
    rows, width = q_ref.shape
    hd = gain_ref.shape[1]

    @pl.when(pl.program_id(0) == 0)
    def _():
        upright_tables(gain_ref, rows_ref, base_ref, scale, held)

    for h in range(width // hd):
        turned = q_ref[:, h * hd : (h + 1) * hd].T
        turned_ref[0, :, h * rows : (h + 1) * rows] = turned
        u = turned.astype(f32)
        inverse = lax.rsqrt(jnp.mean(u * u, axis=0, keepdims=True) + epsilon)
        y = u * inverse * held[2]
        z = y * held[0] + swap_rows(y) * held[1]
        scaled_ref[0, :, h * rows : (h + 1) * rows] = z.astype(bf16)


def share_index(j, half, c, z, core, zs, blocks):
    owner_core = core if half else 1 - core
    return ((z ^ j) * 2 + owner_core) * blocks + c


def arrival_kernel(blocks, zs, dest_hbm, h_hbm, w_hbm, *refs):
    outs, late_outs = refs[:blocks], refs[blocks : 2 * blocks]
    dest_held, h_held, w_held, turned, sems = refs[2 * blocks :]
    me, dp = lax.axis_index("ctx"), lax.axis_index("dp")
    z, core = dp // 2, dp % 2
    parts, rows, part = h_held.shape
    share = turned.shape[0] // (blocks * zs * 2)
    kv_width = w_held.shape[1]
    copies = [pltpu.make_async_copy(dest_hbm, dest_held, sems.at[0])]
    for i in range(parts):
        piece = pl.ds(i * part, part)
        copies.append(pltpu.make_async_copy(h_hbm.at[:, piece], h_held.at[i], sems.at[1 + i]))
    for i in range(parts):
        piece = pl.ds(i * part, part)
        copies.append(
            pltpu.make_async_copy(w_hbm.at[piece], w_held.at[piece], sems.at[1 + parts + i])
        )
    for copy in copies:
        copy.start()
    copies[0].wait()
    marks = place_marks(dest_held, blocks)
    for i in range(parts):
        copies[1 + i].wait()
        for c in range(part // 128):
            at = i * part + c * 128
            turned[at : at + 128] = h_held[i, :, c * 128 : (c + 1) * 128].T
    first = kv_width // 128 * rows + meta_rows
    for m in range(blocks):
        outs[m][first - meta_rows : first] = marks
        c = lax.rem(me + m, blocks)
        for half in range(2):
            for j in range(zs):
                start = share_index(j, half, c, z, core, zs, blocks) * share
                start = pl.multiple_of(start, 16)
                piece = turned[pl.ds(start, share)]
                if half:
                    late_outs[m][j * share : (j + 1) * share] = piece
                else:
                    outs[m][first + j * share : first + (j + 1) * share] = piece
    total = None
    for i in range(parts):
        copies[1 + parts + i].wait()
        product = jnp.dot(
            h_held[i], w_held[i * part : (i + 1) * part], preferred_element_type=f32
        )
        total = product if total is None else total + product
    total = total.astype(bf16)
    for m in range(blocks):
        for h in range(kv_width // 128):
            outs[m][h * rows : (h + 1) * rows] = total[:, h * 128 : (h + 1) * 128]


def mark_rows(ref, rows):
    return ref[rows : rows + meta_rows, :rows].astype(f32)


def arrival_slots(marks, me, blocks, rows):
    marks = marks.astype(f32)
    away = me.astype(f32) - marks[:1]
    away = jnp.where(away < 0, away + blocks, away)
    return away * rows + marks[1:2]


def attend_kernel(back, qs_ref, g_ref, *refs):
    k_refs = refs[: back + 1]
    p_ref, own_ref = refs[back + 1], refs[back + 2]
    send_refs = refs[back + 3 : 2 * back + 3]
    bias_ref = refs[-1]
    rows = g_ref.shape[0]
    hd = own_ref.shape[1]
    group = g_ref.shape[1] // hd

    @pl.when(pl.program_id(0) == 0)
    def _():
        query_doc = mark_rows(k_refs[0], rows)[:1]
        for b in range(back + 1):
            key_doc = jnp.broadcast_to(mark_rows(k_refs[b], rows)[:1], (rows, rows)).T
            allowed = key_doc == query_doc
            if b == 0:
                key_row = lax.broadcasted_iota(jnp.int32, (rows, rows), 0)
                query_row = lax.broadcasted_iota(jnp.int32, (rows, rows), 1)
                allowed = allowed & (key_row <= query_row)
            else:
                allowed = allowed & (lax.axis_index("ctx") >= b)
            bias_ref[b * rows : (b + 1) * rows] = jnp.where(allowed, 0.0, masked)

    keys = jnp.concatenate([r[:rows] for r in k_refs], axis=0)
    logits = jnp.dot(keys, qs_ref[0], preferred_element_type=f32)
    e = jnp.exp2(logits + jnp.concatenate([bias_ref[...]] * group, axis=1))
    p = (e * (1.0 / jnp.sum(e, axis=0, keepdims=True))).astype(bf16)
    p_ref[0] = p
    g = jnp.concatenate([g_ref[:, j * hd : (j + 1) * hd] for j in range(group)], axis=0)
    gv = jnp.dot(p, g, preferred_element_type=f32)
    own_ref[...] = gv[:rows]
    for b in range(back):
        send_refs[b][...] = gv[(b + 1) * rows : (b + 2) * rows].astype(bf16)


def slab_values_kernel(blocks, kv, *refs):
    a_refs, out_ref = refs[:-1], refs[-1]
    me = lax.axis_index("ctx")
    key_count, width = out_ref.shape
    rows = a_refs[0].shape[1]
    first = kv * rows
    slot = lax.broadcasted_iota(jnp.int32, (key_count, rows), 0).astype(f32)
    place, arrived = [], []
    for r in a_refs:
        at = arrival_slots(r[first : first + meta_rows], me, blocks, rows)
        place.append((slot == at).astype(f32).astype(bf16))
        arrived.append(jnp.concatenate([r[h * rows : (h + 1) * rows] for h in range(kv)], axis=1))
    out_ref[...] = jnp.dot(
        jnp.concatenate(place, axis=1), jnp.concatenate(arrived, axis=0), preferred_element_type=f32
    ).astype(bf16)


def backward_kernel(back, factor, p_ref, values_ref, g_ref, u_ref, qs_ref, gain_ref, rows_ref, base_ref, *refs):
    k_refs, refs = refs[: back + 1], refs[back + 1 :]
    gq_ref, own_ref, send_refs, held = refs[0], refs[1], refs[2:-1], refs[-1]
    rows = g_ref.shape[0]
    hd = own_ref.shape[1]
    group = g_ref.shape[1] // hd

    @pl.when(pl.program_id(0) == 0)
    def _():
        upright_tables(gain_ref, rows_ref, base_ref, factor, held)

    g = jnp.concatenate([g_ref[:, j * hd : (j + 1) * hd] for j in range(group)], axis=0)
    dp = lax.dot_general(values_ref[...], g, NT, preferred_element_type=f32)
    p = p_ref[0].astype(f32)
    delta = jnp.sum(p * dp, axis=0, keepdims=True)
    ds = (p * (dp - delta)).astype(bf16)
    gk = lax.dot_general(ds, qs_ref[0], NT, preferred_element_type=f32) * math.log(2.0)
    own_ref[...] = gk[:rows]
    for b in range(back):
        send_refs[b][...] = gk[(b + 1) * rows : (b + 2) * rows].astype(bf16)
    keys = jnp.concatenate([r[:rows] for r in k_refs], axis=0)
    gq = jnp.dot(keys.T, ds, preferred_element_type=f32)
    for j in range(group):
        cols = slice(j * rows, (j + 1) * rows)
        dz, u = gq[:, cols], u_ref[0, :, cols].astype(f32)
        inverse = lax.rsqrt(jnp.mean(u * u, axis=0, keepdims=True) + epsilon)
        dn = (dz * held[0] + swap_rows(dz * held[1])) * held[2]
        along = jnp.mean(dn * u, axis=0, keepdims=True) * (inverse * inverse)
        gq_ref[:, j * hd : (j + 1) * hd] = (inverse * (dn - u * along)).astype(bf16).T


def key_back_kernel(k_ref, own_ref, gain_ref, rows_ref, base_ref, *refs):
    got_refs, out_ref = refs[:-1], refs[-1]
    me = lax.axis_index("ctx")
    hd = gain_ref.shape[1]
    cosine, sine = rotation(rows_ref, base_ref, me)
    total = own_ref[...]
    for r in got_refs:
        total = total + r[...].astype(f32)
    for h in range(k_ref.shape[1] // hd):
        cols = slice(h * hd, (h + 1) * hd)
        u = k_ref[:, cols].astype(f32)
        out_ref[:, cols] = norm_rope_back(u, total[:, cols], gain_ref[...], cosine, sine).astype(bf16)


def gate_kernel(*refs):
    pass


def value_sum_kernel(back, total_ref, *refs):
    got_refs, refs = refs[:back], refs[back:]
    count = len(refs) // 2
    late_refs, grad_ref, send_refs = refs[:count], refs[count], refs[count + 1 :]
    total = total_ref[...]
    for r in got_refs:
        total = total + r[...].astype(f32)
    grad = total.astype(bf16)
    grad_ref[...] = grad
    rows, width = grad.shape
    for late_ref, send_ref in zip(late_refs, send_refs):
        for h in range(width // 128):
            send_ref[h * rows : (h + 1) * rows] = grad[:, h * 128 : (h + 1) * 128]
        send_ref[width // 128 * rows :] = late_ref[...]


def pair_kernel(own_ref, got_ref, first_ref, *send_refs):
    share = first_ref.shape[0]
    first_ref[...] = own_ref[:share] + got_ref[:share].astype(f32)
    for j, ref in enumerate(send_refs, 1):
        at = slice(j * share, (j + 1) * share)
        ref[...] = (own_ref[at] + got_ref[at].astype(f32)).astype(bf16)


def total_kernel(first_ref, *refs):
    total = first_ref[...]
    for r in refs[:-1]:
        total = total + r[...].astype(f32)
    refs[-1][...] = total * (1.0 / (lax.axis_size("ctx") * lax.axis_size("dp")))


def hidden_grad_kernel(v_ref, w_ref, out_ref):
    out_ref[...] = lax.dot_general(
        v_ref[...], w_ref[...], NT, preferred_element_type=f32
    ).astype(bf16)


def sibling_weight_kernel(blocks, *refs):
    h_refs, v_refs = refs[:blocks], refs[blocks : 2 * blocks]
    sibling_ref, arrival_ref = refs[2 * blocks :]
    heads = v_refs[0].shape[1] // 128
    me = lax.axis_index("ctx")
    rows = h_refs[0].shape[1]
    first = h_refs[0].shape[0] - sibling_ref.shape[0]
    slab = [v_refs[0][...]]
    for r in v_refs[1:]:
        slab.append(jnp.concatenate([r[h * rows : (h + 1) * rows] for h in range(heads)], axis=1))
    slab = jnp.concatenate(slab, axis=0)
    slot = lax.broadcasted_iota(jnp.int32, (blocks * rows, rows), 0).astype(f32)
    for s in range(blocks):
        at = arrival_slots(h_refs[s][first - meta_rows : first], me, blocks, rows)
        place = (slot == at).astype(f32).T.astype(bf16)
        arrived = jnp.dot(place, slab, preferred_element_type=f32).astype(bf16)
        arrival_ref[s * rows : (s + 1) * rows] = arrived
    features = jnp.concatenate([r[first:] for r in h_refs], axis=1)
    sibling_ref[...] = jnp.dot(features, arrival_ref[...], preferred_element_type=f32).astype(bf16)


def own_weight_kernel(*refs):
    h_refs, arrival_ref, own_ref = refs[:-2], refs[-2], refs[-1]
    half = own_ref.shape[0]
    features = jnp.concatenate([r[r.shape[0] - half :] for r in h_refs], axis=1)
    own_ref[...] = jnp.dot(features, arrival_ref[...], preferred_element_type=f32)


def on_device(hidden, queries, key_states, out_grad, w_value, q_gain, k_gain, dest_rows, doc_ids):
    hidden, queries, key_states, out_grad = hidden[0], queries[0], key_states[0], out_grad[0]
    rows, width = hidden.shape
    hd = q_gain.shape[0]
    kv_width = key_states.shape[1]
    q_width = queries.shape[1]
    kv = kv_width // hd
    group = q_width // kv_width
    blocks, dp_count = lax.axis_size("ctx"), lax.axis_size("dp")
    zs = dp_count // 2
    back = blocks // 2
    factor = hd ** (-0.5)
    share = width // (blocks * dp_count)
    spread = group * rows
    key_count = (back + 1) * rows
    message = jax.ShapeDtypeStruct((rows + meta_rows, kv_width), bf16)
    rows_table, base_table = (jnp.asarray(t) for t in rope_constants(rows, blocks, hd))
    q_gain, k_gain = q_gain[None], k_gain[None]

    def around(array, m):
        return lax.ppermute(array, "ctx", [(i, (i + m) % blocks) for i in range(blocks)])

    def call(kernel, out_shape, name, operands, mib, flops=0, nbytes=0, in_specs=None, after=(), **kw):
        if in_specs is None:
            in_specs = [pl.BlockSpec(memory_space=VMEM)] * len(operands)
        return pl.pallas_call(
            ordered(kernel, len(operands), len(after)), out_shape=out_shape, name=name,
            compiler_params=params(mib), cost_estimate=cost(flops, nbytes),
            in_specs=list(in_specs) + [pl.BlockSpec(memory_space=pl.ANY)] * len(after), **kw,
        )(*operands, *after)

    def in_hbm(array):
        return pltpu.with_memory_space_constraint(array, pltpu.HBM)

    def gate(arrays, after, name):
        return pl.pallas_call(
            gate_kernel, name=name, compiler_params=params(1), cost_estimate=cost(0, 0),
            out_shape=[jax.ShapeDtypeStruct(a.shape, a.dtype) for a in arrays],
            in_specs=[pl.BlockSpec(memory_space=pl.ANY)] * (len(arrays) + len(after)),
            out_specs=[pl.BlockSpec(memory_space=pl.ANY)] * len(arrays),
            input_output_aliases={i: i for i in range(len(arrays))},
        )(*arrays, *after)

    def whole(shape):
        return pl.BlockSpec(shape, lambda h: (0,) * len(shape))

    sources = [in_hbm(a) for a in (key_states, doc_ids, k_gain, rows_table, base_table)]
    key_own = call(
        key_message_kernel, message, "key_message", sources, 4, 0, 1e6,
        in_specs=[pl.BlockSpec(memory_space=pltpu.HBM)] * 5,
        scratch_shapes=[VMEM(a.shape, a.dtype) for a in sources] + [pltpu.SemaphoreType.DMA((5,))],
    )
    key_messages = [key_own] + [around(key_own, m) for m in range(1, back + 1)]

    head_cols = pl.BlockSpec((rows, group * hd), lambda h: (0, h))
    head_set = pl.BlockSpec((1, hd, spread), lambda h: (h, 0, 0))
    message_cols = pl.BlockSpec((rows + meta_rows, hd), lambda h: (0, h))
    row_cols = pl.BlockSpec((rows, hd), lambda h: (0, h))
    table_specs = [whole((1, hd)), whole(rows_table.shape), whole(base_table.shape)]
    upright = VMEM((3, hd, rows), f32)

    half = width // blocks // 2
    length = kv * rows + meta_rows + half
    sources = [in_hbm(a) for a in (dest_rows, hidden, w_value)]
    if share % 16 == 0:
        arrivals = call(
            functools.partial(arrival_kernel, blocks, zs),
            [jax.ShapeDtypeStruct((length, hd), bf16)] * blocks
            + [jax.ShapeDtypeStruct((half, hd), bf16)] * blocks,
            "arrivals", sources, 24, 2 * rows * width * kv_width, 9e6,
            in_specs=[pl.BlockSpec(memory_space=pltpu.HBM)] * 3, after=(key_own,),
            scratch_shapes=[
                VMEM((1, rows), jnp.int32),
                VMEM((8, rows, width // 8), bf16),
                VMEM((width, kv_width), bf16),
                VMEM((width, rows), bf16),
                pltpu.SemaphoreType.DMA((17,)),
            ],
        )
    else:
        me, dp = lax.axis_index("ctx"), lax.axis_index("dp")
        turned = hidden.T.reshape(dp_count * blocks, share, rows)
        value_own = call(
            value_kernel, jax.ShapeDtypeStruct((rows, kv_width), bf16), "value", sources[1:], 16,
            2 * rows * width * kv_width, 7e6,
            in_specs=[pl.BlockSpec(memory_space=pltpu.HBM)] * 2,
            scratch_shapes=[VMEM(a.shape, a.dtype) for a in sources[1:]]
            + [pltpu.SemaphoreType.DMA((9,))],
        )
        marks = call(
            marks_kernel(blocks), jax.ShapeDtypeStruct((meta_rows, rows), bf16), "marks", (dest_rows,), 1
        )
        head_values = [value_own[:, h * hd : (h + 1) * hd] for h in range(kv)]
        arrivals, late = [], []
        for m in range(blocks):
            at = [
                share_index(j, half, lax.rem(me + m, blocks), dp // 2, dp % 2, zs, blocks)
                for half in range(2)
                for j in range(zs)
            ]
            pieces = [lax.dynamic_index_in_dim(turned, place, axis=0) for place in at]
            pieces = jnp.concatenate(pieces, axis=0).reshape(width // blocks, rows)
            arrivals.append(jnp.concatenate([*head_values, marks, pieces[:half]], axis=0))
            late.append(pieces[half:])
        arrivals = arrivals + late
    arrivals, late = arrivals[:blocks], arrivals[blocks:]
    first_arrival = arrivals[0]
    q_scaled, q_turned = call(
        functools.partial(query_prep_kernel, factor * math.log2(math.e)),
        [jax.ShapeDtypeStruct((kv, hd, spread), bf16)] * 2,
        "query_prep", (queries, q_gain, rows_table, base_table), 8, 0, 4e6, grid=(kv,),
        in_specs=[head_cols] + table_specs, out_specs=[head_set] * 2, scratch_shapes=[upright],
        after=(first_arrival,),
    )

    leaving = gate(arrivals[1:], tuple(key_messages[1:]), "arrivals_leave")
    arrivals = [first_arrival] + [around(leaving[m - 1], m) for m in range(1, blocks)]

    attended = call(
        functools.partial(attend_kernel, back),
        [
            jax.ShapeDtypeStruct((kv, key_count, spread), bf16),
            jax.ShapeDtypeStruct((rows, kv_width), f32),
        ]
        + [jax.ShapeDtypeStruct((rows, kv_width), bf16)] * back,
        "attend", (q_scaled, out_grad, *key_messages), 16,
        8 * kv * key_count * spread * hd, 5e6, grid=(kv,),
        in_specs=[head_set, head_cols] + [message_cols] * (back + 1),
        out_specs=[pl.BlockSpec((1, key_count, spread), lambda h: (h, 0, 0))]
        + [row_cols] * (back + 1),
        scratch_shapes=[VMEM((key_count, rows), f32)], after=(leaving[0],),
    )
    probabilities, value_total = attended[0], attended[1]
    value_got = [around(attended[1 + m], blocks - m) for m in range(1, back + 1)]

    slab_values = call(
        functools.partial(slab_values_kernel, blocks, kv),
        jax.ShapeDtypeStruct((key_count, kv_width), bf16), "slab_values", arrivals, 16,
        2 * key_count * blocks * rows * kv_width, 2e6, after=(value_total,),
    )
    value_grad, *followed = call(
        functools.partial(value_sum_kernel, back),
        [jax.ShapeDtypeStruct((rows, kv_width), bf16)]
        + [jax.ShapeDtypeStruct((kv * rows + half, hd), bf16)] * (blocks - 1),
        "value_sum", (value_total, *value_got, *late[1:]), 8, 0, 3e6, after=(slab_values,),
    )
    followed = [around(followed[m - 1], m) for m in range(1, blocks)]

    backed = call(
        functools.partial(backward_kernel, back, factor),
        [
            jax.ShapeDtypeStruct((rows, q_width), bf16),
            jax.ShapeDtypeStruct((rows, kv_width), f32),
        ]
        + [jax.ShapeDtypeStruct((rows, kv_width), bf16)] * back,
        "backward",
        (
            probabilities, slab_values, out_grad, q_turned, q_scaled, q_gain, rows_table, base_table,
            *key_messages,
        ),
        20, 12 * kv * key_count * spread * hd, 7e6, grid=(kv,),
        in_specs=[
            pl.BlockSpec((1, key_count, spread), lambda h: (h, 0, 0)),
            pl.BlockSpec((key_count, hd), lambda h: (0, h)),
            head_cols, head_set, head_set,
        ]
        + table_specs + [message_cols] * (back + 1),
        out_specs=[head_cols] + [row_cols] * (back + 1),
        scratch_shapes=[upright],
        after=(value_grad,),
    )
    sibling, arrival = call(
        functools.partial(sibling_weight_kernel, blocks),
        [
            jax.ShapeDtypeStruct((half, kv_width), bf16),
            jax.ShapeDtypeStruct((blocks * rows, kv_width), bf16),
        ],
        "sibling_weight", (*arrivals, value_grad, *followed), 16, width * rows * kv_width, 4e6,
        after=(backed[1],),
    )
    own = call(
        own_weight_kernel, jax.ShapeDtypeStruct((half, kv_width), f32), "own_weight",
        (late[0], *followed, arrival), 16, width * rows * kv_width, 3e6,
    )
    got = lax.ppermute(sibling, "dp", [(d, d ^ 1) for d in range(dp_count)])

    slice_width = width // 4
    hidden_grad = call(
        hidden_grad_kernel, jax.ShapeDtypeStruct((rows, width), bf16),
        "hidden_grad", (value_grad, w_value), 8, 2 * rows * width * kv_width, 7e6,
        grid=(width // slice_width,),
        in_specs=[whole((rows, kv_width)), pl.BlockSpec((slice_width, kv_width), lambda i: (i, 0))],
        out_specs=pl.BlockSpec((rows, slice_width), lambda i: (0, i)),
        after=(),
    )

    pairs = call(
        pair_kernel,
        [jax.ShapeDtypeStruct((share, kv_width), f32)]
        + [jax.ShapeDtypeStruct((share, kv_width), bf16)] * (zs - 1),
        "pair", (own, got), 12, 0, 3e6,
    )
    sums = []
    for j in range(zs - 1, 0, -1):
        route = [(z * 2 + c, (z ^ j) * 2 + c) for z in range(zs) for c in range(2)]
        sums.append(lax.ppermute(pairs[j], "dp", route))

    query_grad = backed[0]
    key_leaving = gate(backed[2:], (pairs[0],), "keys_leave")
    key_got = [around(key_leaving[m - 1], blocks - m) for m in range(1, back + 1)]
    weight_grad = call(
        total_kernel, jax.ShapeDtypeStruct((share, kv_width), f32), "total",
        (pairs[0], *sums), 4, 0, 1e6,
    )
    key_grad = call(
        key_back_kernel, jax.ShapeDtypeStruct((rows, kv_width), bf16), "key_back",
        (key_states, backed[1], k_gain, rows_table, base_table, *key_got), 4, 0, 1e6,
    )
    return (hidden_grad[None], query_grad[None], key_grad[None], weight_grad)


def solution(mesh):
    return jax.shard_map(
        on_device,
        mesh=mesh,
        in_specs=(
            P("dp", "ctx", None),
            P("dp", "ctx", None),
            P("dp", "ctx", None),
            P("dp", "ctx", None),
            P(),
            P(),
            P(),
            P("dp", "ctx"),
            P("dp", "ctx"),
        ),
        out_specs=(
            P("dp", "ctx", None),
            P("dp", "ctx", None),
            P("dp", "ctx", None),
            P(("dp", "ctx"), None),
        ),
        check_vma=False,
    )
```
